256 devices in a mesh: tile: 32 (over x, z), depth: 8 (over y, core).
Axes of the slice: x: 4, y: 4, z: 8, core: 2. Of those that a mesh axis runs over, the one named last changes fastest.
Arguments:
- perturbation: float32 [4, 32, 1024, 128], P(None, 'depth', 'tile'), may hold values from -6 to 6
- cotangent: float32 [4, 32, 1024, 128], P(None, 'depth', 'tile'), may hold values from -6 to 6
- land_mask: int32 [1024, 128], P('tile'), may hold values 0 or 1
- bottom_level: int32 [1024, 128], P('tile'), may hold values from 1 to 32
- mix_gain: float32 [32, 1024, 128], P('depth', 'tile'), may hold values from 0.5 to 1.5
- expansion: float32 [32, 1024, 128], P('depth', 'tile'), may hold values from 0.1 to 1
- contraction: float32 [32, 1024, 128], P('depth', 'tile'), may hold values from 0.1 to 1
- columns: int32 [131072], P('tile'), may hold values from 0 to 4095
- owners: int32 [131072, 1], P('tile'), may hold values from 0 to 31; in each aligned block of 4096 rows (0 to 4095, 4096 to 8191, ...) at most 256 rows name the same one
- level_start: int32 [131072], P('tile'), may hold values from 0 to 15
- level_count: int32 [131072], P('tile'), may hold values from 1 to 16
Outputs:
- final_state: float32 [4, 32, 1024, 128], P(None, 'depth', 'tile')
- adjoint_state: float32 [4, 32, 1024, 128], P(None, 'depth', 'tile')
- profiles: float32 [4, 32, 32, 8192], P(None, 'depth', 'tile')
- sensitivity: float32 [32, 8192], P('tile')
The draws below stay inside these ranges and needn't reach their ends.
Inputs may be any that keep to these rules, and one draw needn't show every extreme that they name: `owners`: among the 4096 candidates listed by one tile, no owner is named more than 256 times; some owner is named exactly 256 times by some tile.
All inputs are finite; a program needn't handle non-finite values. No bound on the sum of `land_mask` on one device may be relied on, other than what follows from the above.
Results may differ from the reference program's by a relative error of at most 0.00002.
Values sent between devices are 32-bit elements; how exact they have to be, the bound alone decides.
A program may use at most 64 MiB of HBM per device.

```python
import math
import jax
import jax.numpy as jnp
import numpy as np
from jax import lax

LON = 128
ROWS_DEV = 32
CAND_DEV = 4096
STEPS = 2
NY = 1024
LEVELS = 32
CANDIDATES = 131072
CAP = 256
N_TILE = 32


def place_ends(result, key, smallest, largest):
    place = [jax.random.randint(jax.random.fold_in(key, axis), (), 0, length) for axis, length in enumerate(result.shape)]
    main_axis = result.shape.index(max(result.shape))
    neighbour = place[:main_axis] + [(place[main_axis] + 1) % result.shape[main_axis]] + place[main_axis + 1:]
    return result.at[tuple(place)].set(smallest).at[tuple(neighbour)].set(largest)


def levels(key, extent, cuts, least, high):
    loudness = 1.0
    for position, blocks in cuts:
        steps = jax.random.uniform(jax.random.fold_in(jax.random.fold_in(key, 6), position), (blocks,), jnp.float32, least / len(cuts), high / len(cuts))
        loudness = loudness * jnp.repeat(jnp.exp(steps), extent[position] // blocks).reshape((-1,) + (1,) * (len(extent) - 1 - position))
    return loudness


def routed_block(rng, own, number, rows, number_of, top, most, lean):
    ranking = jax.random.permutation(rng, number_of)
    crowded, ordinary = load_shares(number_of, rows * top, most, lean, True), load_shares(number_of, rows * top, most, lean, False)
    places = jnp.arange(number_of)

    def named(sizes, turn):
        used = int((sizes > 0).sum())
        fixed = max(1, used // 4)
        passed = fixed + (places - fixed + turn * (used - fixed)) % max(1, number_of - fixed)
        return jnp.zeros((number_of,), jnp.int32).at[ranking[jnp.where(places < fixed, places, passed)]].set(jnp.asarray(sizes, jnp.int32))

    sizes = jnp.where(number % 4 == 0, named(crowded, number // 4), named(ordinary, number - number // 4 - 1))
    mixed = jax.random.permutation(jax.random.fold_in(own, 3), number_of)
    source_of, sink = mixed[0:number_of // 2 * 2:2], mixed[1:number_of // 2 * 2:2]
    room = jnp.minimum(sizes[source_of] - 1, most - sizes[sink]) // 2
    room = jnp.where((source_of == ranking[0]) | (sink == ranking[0]) | (sizes[sink] == 0), 0, jnp.maximum(room, 0))
    passed = jax.random.randint(jax.random.fold_in(own, 4), (number_of // 2,), 0, 1 << 20) % (room + 1)
    sizes = sizes.at[source_of].add(-passed).at[sink].add(passed)
    items = jnp.searchsorted(jnp.cumsum(sizes), jnp.arange(rows * top), side="right").astype(jnp.int32)
    table = items.reshape(top, rows).T
    table = table[jax.random.permutation(jax.random.fold_in(own, 1), rows)]
    turn = jax.random.randint(jax.random.fold_in(own, 2), (rows, 1), 0, top)
    return jnp.take_along_axis(table, (jnp.arange(top)[None, :] + turn) % top, axis=1)


def load_shares(amount, total, limit, slope, full):
    portions = [(1 << 20) // math.isqrt(standing ** slope) + 1 for standing in range(1, amount + 1)]
    largest = limit if full else min(limit, max(-(-total // amount), total * portions[0] // sum(portions)))
    least = 1 if total - largest >= amount - 1 else 0
    counts, rest = [largest] + [least] * (amount - 1), total - largest - least * (amount - 1)
    while rest > 0:
        candidates = [i for i in range(1, amount) if counts[i] < largest] or [i for i in range(1, amount) if counts[i] < limit]
        pool, budget = sum([portions[i] for i in candidates]), rest
        for i in candidates:
            more = min(limit - counts[i], max(1, budget * portions[i] // pool), rest)
            counts[i] = counts[i] + more
            rest = rest - more
    return np.array(counts)


def centred(stream_key, extent, scale, reach, cuts=(), kind=jnp.bfloat16):
    array = jax.random.normal(stream_key, extent, jnp.float32) * scale
    if len(cuts) > 0:
        array = levels(stream_key, extent, cuts, -0.22, 0.18) * array
    return jnp.clip(array, min=-reach, max=reach).astype(kind)


def setup_inputs(seed: int = 0) -> dict:
    keys = jax.random.split(jax.random.key(seed), 12)
    perturbation = centred(keys[0], (4, LEVELS, NY, LON), 1.0, 6.0, ((1, 8), (2, 32)), jnp.float32)
    cotangent = centred(keys[1], (4, LEVELS, NY, LON), 1.0, 6.0, ((1, 8), (2, 32)), jnp.float32)
    land_mask = place_ends((jax.random.randint(keys[2], (NY, LON), 0, 5) < 4).astype(jnp.int32), jax.random.fold_in(keys[2], 1), 0, 1)
    bottom_level = place_ends(jax.random.randint(keys[3], (NY, LON), 1, LEVELS + 1), jax.random.fold_in(keys[3], 1), 1, LEVELS).astype(jnp.int32)
    mix_gain = jnp.clip(jnp.exp(math.log(1.5) - 1.0986123 * jax.random.uniform(keys[4], (LEVELS, NY, LON), jnp.float32) ** levels(keys[4], (LEVELS, NY, LON), ((0, 8), (1, 32)), -0.2, 0.2)), 0.5, 1.5)
    expansion = jnp.clip(jnp.exp(math.log(1.0) - 2.3025851 * jax.random.uniform(keys[5], (LEVELS, NY, LON), jnp.float32) ** levels(keys[5], (LEVELS, NY, LON), ((0, 8), (1, 32)), -0.2, 0.2)), 0.1, 1.0)
    contraction = jnp.clip(jnp.exp(math.log(1.0) - 2.3025851 * jax.random.uniform(keys[6], (LEVELS, NY, LON), jnp.float32) ** levels(keys[6], (LEVELS, NY, LON), ((0, 8), (1, 32)), -0.2, 0.2)), 0.1, 1.0)
    columns = place_ends(jax.random.randint(keys[7], (CANDIDATES,), 0, ROWS_DEV * LON), jax.random.fold_in(keys[7], 1), 0, (ROWS_DEV * LON) - 1).astype(jnp.int32)
    owners_keys = jax.random.split(jax.random.fold_in(keys[8], 1), CANDIDATES // CAND_DEV)
    owners_turns = jax.random.permutation(jax.random.fold_in(keys[8], 3), CANDIDATES // CAND_DEV)
    owners = jax.vmap(lambda own, number: routed_block(jax.random.fold_in(keys[8], 2), own, number, CAND_DEV, N_TILE, 1, CAP, 2))(owners_keys, owners_turns).reshape((CANDIDATES, 1))
    level_start = place_ends(jax.random.randint(keys[9], (CANDIDATES,), 0, LEVELS // 2), jax.random.fold_in(keys[9], 1), 0, (LEVELS // 2) - 1).astype(jnp.int32)
    level_count = place_ends(jax.random.randint(keys[10], (CANDIDATES,), 1, LEVELS // 2 + 1), jax.random.fold_in(keys[10], 1), 1, (LEVELS // 2 + 1) - 1).astype(jnp.int32)
    return dict(perturbation=perturbation, cotangent=cotangent, land_mask=land_mask, bottom_level=bottom_level, mix_gain=mix_gain, expansion=expansion, contraction=contraction, columns=columns, owners=owners, level_start=level_start, level_count=level_count)


nu_horiz = 0.06
nu_vert = 0.08
press_coef = 0.1
grav_step = 0.2
sens_scale = 0.2

def spread(padded):
    center = padded[:, 1:-1, 1:-1]
    horizontal = padded[:, 1:-1, 2:] + padded[:, 1:-1, :-2] + jnp.roll(center, 1, 3) + jnp.roll(center, -1, 3) - 4.0 * center
    vertical = padded[:, 2:, 1:-1] + padded[:, :-2, 1:-1] - 2.0 * center
    return nu_horiz * horizontal + nu_vert * vertical

def east_diff(field):
    return 0.5 * (jnp.roll(field, -1, 2) - jnp.roll(field, 1, 2))

def north_diff(padded_field):
    return 0.5 * (padded_field[1:-1, 2:] - padded_field[1:-1, :-2])

def rotation(row_ids, total_rows):
    return 0.4 * jnp.sin(math.pi * ((row_ids.astype(jnp.float32) + 0.5) / total_rows - 0.5))

def advance(fields, wet_mask, mix_gain, expansion, contraction, coriolis):
    pressure = grav_step * jnp.cumsum(contraction * fields[1] - expansion * fields[0], 0)
    stacked = jnp.concatenate([wet_mask * mix_gain * fields, pressure[None]], 0)
    padded = jnp.pad(stacked, ((0, 0), (1, 1), (1, 1), (0, 0)))
    mixing = mix_gain * wet_mask * spread(padded[:4])
    new_temp = fields[0] + mixing[0]
    new_salt = fields[1] + mixing[1]
    new_east = fields[2] + mixing[2] + coriolis * fields[3] - press_coef * east_diff(pressure)
    new_north = fields[3] + mixing[3] - coriolis * fields[2] - press_coef * north_diff(padded[4])
    return wet_mask * jnp.stack([new_temp, new_salt, new_east, new_north], 0)

def reference(perturbation, cotangent, land_mask, bottom_level, mix_gain, expansion, contraction, columns, owners, level_start, level_count):
    levels_all = perturbation.shape[1]
    rows_all = perturbation.shape[2]
    width = perturbation.shape[3]
    level_ids = jnp.arange(levels_all, dtype=jnp.int32)
    wet_mask = ((land_mask[None] == 1) & (level_ids[:, None, None] < bottom_level[None])).astype(jnp.float32)
    coriolis = rotation(jnp.arange(rows_all, dtype=jnp.int32), rows_all)[None, :, None]

    def window(fields):
        for repeat in range(STEPS):
            fields = advance(fields, wet_mask, mix_gain, expansion, contraction, coriolis)
        return fields
    final_state, pullback = jax.vjp(window, perturbation)
    adjoint_state = pullback(cotangent)[0]
    tile_count = N_TILE
    capacity = 2 * CAND_DEV // tile_count
    owner_flat = owners[:, 0]
    onehot = (owner_flat.reshape(tile_count, CAND_DEV)[:, :, None] == jnp.arange(tile_count, dtype=jnp.int32)[None, None, :]).astype(jnp.int32)
    slot_rank = lax.optimization_barrier(jnp.sum((jnp.cumsum(onehot, 1) - 1) * onehot, 2)).reshape(-1)
    source = jnp.arange(tile_count * CAND_DEV, dtype=jnp.int32) // CAND_DEV
    slot_ids = source * capacity + slot_rank
    global_cols = source * (ROWS_DEV * LON) + columns
    kept_mask = ((level_ids[:, None] >= level_start[None]) & (level_ids[:, None] < (level_start + level_count)[None])).astype(jnp.float32)
    picked = final_state.reshape(4, levels_all, rows_all * width)[:, :, global_cols]
    kept_vals = picked * kept_mask[None]
    adjoint_picked = adjoint_state.reshape(4, levels_all, rows_all * width)[:, :, global_cols]
    partial_value = sens_scale * lax.optimization_barrier(jnp.sum(adjoint_picked * kept_vals, (0, 1)))
    profiles = jnp.zeros((4, levels_all, tile_count, tile_count * capacity), jnp.float32).at[:, :, owner_flat, slot_ids].set(kept_vals)
    sensitivity = jnp.zeros((tile_count, tile_count * capacity), jnp.float32).at[owner_flat, slot_ids].set(partial_value)
    return (final_state, adjoint_state, profiles, sensitivity)
```

```python
import functools
import math

import jax
import jax.numpy as jnp
from jax import lax
from jax.experimental import pallas as pl
from jax.experimental.pallas import tpu as pltpu
from jax.sharding import PartitionSpec as P

STEPS = 2
LANES = 128

nu_horiz = 0.06
nu_vert = 0.08
press_coef = 0.1
grav_step = 0.2
sens_scale = 0.2

MESH = pl.DeviceIdType.MESH
F32 = jnp.float32
BF16 = jnp.bfloat16
I32 = jnp.int32


def iota(shape, dim):
    return lax.broadcasted_iota(I32, shape, dim)


def lane_diff(p):
    return 0.5 * (pltpu.roll(p, p.shape[1] - 1, 1) - pltpu.roll(p, 1, 1))


def row_after(p, bottom):
    rows = p.shape[0]
    return jnp.where(iota(p.shape, 0) == rows - 1, bottom, pltpu.roll(p, rows - 1, 0))


def row_before(p, top):
    return jnp.where(iota(p.shape, 0) == 0, top, pltpu.roll(p, 1, 0))


def kernel(
    tiles,
    depths,
    pert,
    cot,
    land,
    bottom,
    gain,
    expan,
    contr,
    cols,
    owns,
    starts,
    counts,
    fin_out,
    adj_out,
    prof_out,
    sens_out,
    wet,
    gw,
    fin,
    mid,
    amid,
    act,
    qf,
    qb,
    runs,
    edge_out,
    edge_in,
    tot_out,
    tot_in,
    diag_out,
    diag_in,
    rank_in,
    ranks,
    hot_own,
    hot_rank,
    lane_tab,
    row_tab,
    lev_tab,
    cells,
    sens_cells,
    send_buf,
    sens_part,
    sens_peer,
    sens_send,
    q_send,
    q_recv,
    e_send,
    e_recv,
    t_send,
    t_recv,
    d_send,
    d_recv,
    p_sem,
    s_sem,
    x_send,
    x_recv,
):
    levels, rows = wet.shape[0], wet.shape[1]
    cap = ranks_cap = hot_rank.shape[0]
    halves = cap // LANES
    chunks = owns.shape[0]
    planes = 4 * levels
    t = lax.axis_index("tile")
    d = lax.axis_index("depth")

    barrier = pltpu.get_barrier_semaphore()

    def greet(to_tile, to_depth):
        pl.semaphore_signal(barrier, inc=1, device_id=(to_tile, to_depth), device_id_type=MESH)

    def greet_depths(j, _):
        peer = lax.rem(d + j, depths)
        greet(t, peer)

        @pl.when(t > 0)
        def _():
            greet(t - 1, peer)

        @pl.when(t < tiles - 1)
        def _():
            greet(t + 1, peer)

        return 0

    lax.fori_loop(1, depths, greet_depths, 0)

    def greet_tiles(j, _):
        greet(lax.rem(t + j, tiles), d)
        return 0

    lax.fori_loop(1, tiles, greet_tiles, 0)

    zero_plane = jnp.zeros((rows, LANES), F32)
    ocean = land[...] == 1
    for k in range(levels):
        w = jnp.where(ocean & (d * levels + k < bottom[...]), 1.0, 0.0).astype(F32)
        wet[k] = w
        gw[k] = w * gain[k]

    @pl.when(d == 0)
    def _():
        for s in range(2):
            for f in range(4):
                qf[s, f, 0] = zero_plane
                qb[s, f, 0] = zero_plane

    @pl.when(d == depths - 1)
    def _():
        for s in range(2):
            for f in range(4):
                qf[s, f, levels + 1] = zero_plane
                qb[s, f, levels + 1] = zero_plane

    def clear_side(side):
        for rnd in range(4):
            edge_in[rnd, side] = jnp.zeros(edge_in.shape[2:], F32)
            diag_in[rnd, side] = jnp.zeros(diag_in.shape[2:], F32)

    @pl.when(t == 0)
    def _():
        clear_side(0)

    @pl.when(t == tiles - 1)
    def _():
        clear_side(1)

    def store_edges(rnd, at, plane):
        edge_out[rnd, 0, at : at + 1] = plane[0:1]
        edge_out[rnd, 1, at : at + 1] = plane[rows - 1 : rows]

    def prepare_forward(src, s, rnd):
        running = zero_plane
        for k in range(levels):
            running = running + (contr[k] * src[1, k] - expan[k] * src[0, k])
            runs[rnd, k] = running
            store_edges(rnd, planes + k, running)
        tot_out[rnd] = running
        diag_out[rnd, 0] = running[0:1]
        diag_out[rnd, 1] = running[rows - 1 : rows]
        for f in range(4):
            for k in range(levels):
                q = gw[k] * src[f, k]
                qf[s, f, k + 1] = q
                store_edges(rnd, f * levels + k, q)

    def prepare_backward(src, s, rnd):
        run_u = zero_plane
        run_v = zero_plane
        zero_row = jnp.zeros((1, LANES), F32)
        for k in reversed(range(levels)):
            run_u = run_u + wet[k] * src[2, k]
            run_v = run_v + wet[k] * src[3, k]
            store_edges(rnd, planes + k, run_v)
            runs[rnd, k] = lane_diff(run_u) + 0.5 * (
                row_after(run_v, zero_row) - row_before(run_v, zero_row)
            )
        tot_out[rnd] = runs[rnd, 0]
        diag_out[rnd, 0] = run_v[0:1]
        diag_out[rnd, 1] = run_v[rows - 1 : rows]
        for f in range(4):
            for k in range(levels):
                a = wet[k] * src[f, k]
                act[s, f, k] = a
                q = gw[k] * a
                qb[s, f, k + 1] = q
                store_edges(rnd, f * levels + k, q)

    def remote(src, dst, send, recv, to_tile, to_depth):
        return pltpu.make_async_remote_copy(
            src_ref=src,
            dst_ref=dst,
            send_sem=send,
            recv_sem=recv,
            device_id=(to_tile, to_depth),
            device_id_type=MESH,
        )

    def level_up(q, s, rnd):
        return remote(
            q.at[s, :, levels], q.at[s, :, 0], q_send.at[rnd, 1], q_recv.at[rnd, 0], t, d + 1
        )

    def level_down(q, s, rnd):
        return remote(
            q.at[s, :, 1], q.at[s, :, levels + 1], q_send.at[rnd, 0], q_recv.at[rnd, 1], t, d - 1
        )

    def edge_copy(rnd, side):
        return remote(
            edge_out.at[rnd, side],
            edge_in.at[rnd, 1 - side],
            e_send.at[rnd, side],
            e_recv.at[rnd, 1 - side],
            t - 1 if side == 0 else t + 1,
            d,
        )

    def tot_copy(rnd, peer, slot):
        return remote(
            tot_out.at[rnd], tot_in.at[rnd, slot], t_send.at[rnd, peer], t_recv.at[rnd, slot], t, peer
        )

    def diag_copy(rnd, side, peer, slot):
        return remote(
            diag_out.at[rnd, side],
            diag_in.at[rnd, 1 - side, slot],
            d_send.at[rnd, side, peer],
            d_recv.at[rnd, 1 - side, slot],
            t - 1 if side == 0 else t + 1,
            peer,
        )

    has_side = (t > 0, t < tiles - 1)

    def ahead(forward):
        return (d + 1, depths) if forward else (0, d)

    def behind(forward):
        return (0, d) if forward else (d + 1, depths)

    def send_round(q, s, rnd, forward):
        @pl.when(d < depths - 1)
        def _():
            level_up(q, s, rnd).start()

        @pl.when(d > 0)
        def _():
            level_down(q, s, rnd).start()

        def one(peer, _):
            tot_copy(rnd, peer, d).start()
            for side in range(2):

                @pl.when(has_side[side])
                def _():
                    diag_copy(rnd, side, peer, d).start()

            return 0

        for side in range(2):

            @pl.when(has_side[side])
            def _():
                edge_copy(rnd, side).start()

        lax.fori_loop(*ahead(forward), one, 0)

    def recv_round(q, s, rnd, forward):
        def one(peer, _):
            tot_copy(rnd, peer, peer).wait_recv()
            for side in range(2):

                @pl.when(has_side[1 - side])
                def _():
                    diag_copy(rnd, side, peer, peer).wait_recv()

            return 0

        lax.fori_loop(*behind(forward), one, 0)
        for side in range(2):

            @pl.when(has_side[1 - side])
            def _():
                edge_copy(rnd, side).wait_recv()

        @pl.when(d > 0)
        def _():
            level_up(q, s, rnd).wait_recv()

        @pl.when(d < depths - 1)
        def _():
            level_down(q, s, rnd).wait_recv()

    def drain_round(q, s, rnd, forward):
        def one(peer, _):
            tot_copy(rnd, peer, d).wait_send()
            for side in range(2):

                @pl.when(has_side[side])
                def _():
                    diag_copy(rnd, side, peer, d).wait_send()

            return 0

        lax.fori_loop(*ahead(forward), one, 0)
        for side in range(2):

            @pl.when(has_side[side])
            def _():
                edge_copy(rnd, side).wait_send()

        @pl.when(d < depths - 1)
        def _():
            level_up(q, s, rnd).wait_send()

        @pl.when(d > 0)
        def _():
            level_down(q, s, rnd).wait_send()

    def base_sums(rnd, forward):
        def one(peer, carry):
            base, top, low = carry
            return (
                base + tot_in[rnd, peer],
                top + diag_in[rnd, 0, peer],
                low + diag_in[rnd, 1, peer],
            )

        zero_row = jnp.zeros((1, LANES), F32)
        return lax.fori_loop(*behind(forward), one, (zero_plane, zero_row, zero_row))

    def mixed(q, s, rnd, f, k):
        c = q[s, f, k + 1]
        at = f * levels + k
        north = row_after(c, edge_in[rnd, 1, at : at + 1])
        south = row_before(c, edge_in[rnd, 0, at : at + 1])
        horizontal = (
            north + south + pltpu.roll(c, 1, 1) + pltpu.roll(c, LANES - 1, 1) - 4.0 * c
        )
        vertical = q[s, f, k + 2] + q[s, f, k] - 2.0 * c
        return gw[k] * (nu_horiz * horizontal + nu_vert * vertical)

    row_ids = (t * rows + iota((rows, LANES), 0)).astype(F32)
    coriolis = 0.4 * jnp.sin(math.pi * ((row_ids + 0.5) / (tiles * rows) - 0.5))

    def finish_forward(src, s, rnd, store):
        base, top, low = base_sums(rnd, True)
        for k in range(levels):
            at = planes + k
            p = grav_step * (base + runs[rnd, k])
            p_top = grav_step * (top + edge_in[rnd, 0, at : at + 1])
            p_low = grav_step * (low + edge_in[rnd, 1, at : at + 1])
            gy = 0.5 * (row_after(p, p_low) - row_before(p, p_top))
            w = wet[k]
            for f in range(2):
                store(f, k, w * (src[f, k] + mixed(qf, s, rnd, f, k)))
            u, v = src[2, k], src[3, k]
            store(2, k, w * (u + mixed(qf, s, rnd, 2, k) + coriolis * v - press_coef * lane_diff(p)))
            store(3, k, w * (v + mixed(qf, s, rnd, 3, k) - coriolis * u - press_coef * gy))

    def finish_backward(s, rnd, store):
        base, top, low = base_sums(rnd, False)
        for k in range(levels):
            at = planes + k
            v_top = top + edge_in[rnd, 0, at : at + 1]
            v_low = low + edge_in[rnd, 1, at : at + 1]
            row = iota((rows, LANES), 0)
            rim = jnp.where(row == 0, -0.5 * v_top, 0.0) + jnp.where(row == rows - 1, 0.5 * v_low, 0.0)
            dens = (grav_step * press_coef) * (base + runs[rnd, k] + rim)
            a_t, a_s, a_u, a_v = (act[s, f, k] for f in range(4))
            store(0, k, a_t + mixed(qb, s, rnd, 0, k) - expan[k] * dens)
            store(1, k, a_s + mixed(qb, s, rnd, 1, k) + contr[k] * dens)
            store(2, k, a_u + mixed(qb, s, rnd, 2, k) - coriolis * a_v)
            store(3, k, a_v + mixed(qb, s, rnd, 3, k) + coriolis * a_u)

    prepare_forward(pert, 0, 0)
    prepare_backward(cot, 0, 1)

    sides = has_side[0].astype(I32) + has_side[1].astype(I32)
    pl.semaphore_wait(barrier, (depths - 1) * (1 + sides) + tiles - 1)

    send_round(qf, 0, 0, True)
    send_round(qb, 0, 1, False)

    own_ids = iota((tiles, LANES), 0)

    def rank_inputs(i, before):
        hot = (owns[pl.ds(i, 1), :] == own_ids).astype(F32)
        at = pl.multiple_of(i * tiles, tiles)
        rank_in[pl.ds(at, tiles), 0:LANES] = hot.astype(BF16)
        rank_in[pl.ds(at, tiles), LANES : 2 * LANES] = before.astype(BF16)
        return before + hot

    lax.fori_loop(0, chunks, rank_inputs, jnp.zeros((tiles, LANES), F32))
    i_row, i_col = iota((2 * LANES, LANES), 0), iota((2 * LANES, LANES), 1)
    earlier = jnp.where((i_row < i_col) | (i_row >= LANES), 1.0, 0.0).astype(BF16)
    ranks[...] = jnp.dot(rank_in[...], earlier, preferred_element_type=F32)
    slot_ids = iota((cap, LANES), 0)

    def slot_inputs(i, _):
        hot = (owns[pl.ds(i, 1), :] == own_ids).astype(F32)
        at = pl.multiple_of(i * tiles, tiles)
        lanes = pl.ds(pl.multiple_of(i * LANES, LANES), LANES)
        rank = jnp.sum(hot * ranks[pl.ds(at, tiles), :], axis=0, keepdims=True).astype(I32)
        hot_rank[:, lanes] = (slot_ids == rank).astype(F32).astype(BF16)
        c = cols[pl.ds(i, 1), :]
        lane = (c & (LANES - 1)).astype(F32)
        row = ((c >> 7) + 32).astype(F32)
        lev = (starts[pl.ds(i, 1), :] * 16 + counts[pl.ds(i, 1), :] - 1).astype(F32)
        hot_own[0:tiles, lanes] = (hot * lane).astype(BF16)
        hot_own[tiles : 2 * tiles, lanes] = (hot * row).astype(BF16)
        hot_own[2 * tiles : 3 * tiles, lanes] = (hot * lev).astype(BF16)
        return 0

    lax.fori_loop(0, chunks, slot_inputs, 0)
    table = lax.dot_general(
        hot_own[...], hot_rank[...], (((1,), (1,)), ((), ())), preferred_element_type=F32
    ).astype(I32)
    for h in range(halves):
        part = table[:, h * LANES : (h + 1) * LANES]
        lane_tab[h * tiles : (h + 1) * tiles] = part[0:tiles]
        row_tab[h * tiles : (h + 1) * tiles] = part[tiles : 2 * tiles] - 32
        lev_tab[h * tiles : (h + 1) * tiles] = part[2 * tiles : 3 * tiles]

    def store_mid(f, k, value):
        mid[f, k] = value

    def store_fin(f, k, value):
        fin_out[f, k] = value
        fin[(f * levels + k) * rows : (f * levels + k + 1) * rows] = value

    def store_amid(f, k, value):
        amid[f, k] = value

    def store_adj(f, k, value):
        adj_out[f, k] = value

    recv_round(qf, 0, 0, True)
    finish_forward(pert, 0, 0, store_mid)
    prepare_forward(mid, 1, 2)
    send_round(qf, 1, 2, True)
    recv_round(qb, 0, 1, False)
    finish_backward(0, 1, store_amid)
    prepare_backward(amid, 1, 3)
    send_round(qb, 1, 3, False)
    recv_round(qf, 1, 2, True)
    finish_forward(mid, 1, 2, store_fin)

    groups = planes // 8
    for g in range(groups):
        for r in range(rows):
            cells[r, g * 8 : g * 8 + 8] = fin[pl.ds(g * 8 * rows + r, 8, stride=rows), :]

    sub = iota((8, LANES), 0)
    level_ids = d * levels + lax.rem(sub, levels)

    def profile_copy(owner):
        return remote(
            send_buf.at[owner],
            prof_out.at[:, pl.ds(pl.multiple_of(t * cap, LANES), cap)],
            p_sem.at[0],
            p_sem.at[1],
            owner,
            d,
        )

    def gather_owner(j, _):
        owner = lax.rem(t + j, tiles)
        for h in range(halves):
            at = pl.ds(h * tiles + owner, 1)
            lane = jnp.broadcast_to(lane_tab[at, :], (8, LANES))
            row = jnp.broadcast_to(row_tab[at, :], (8, LANES))
            lev = jnp.broadcast_to(lev_tab[at, :], (8, LANES))
            first = lev >> 4
            kept = (level_ids >= first) & (level_ids <= first + (lev & 15))
            row = jnp.where(kept, row, -1)
            totals = [jnp.zeros((8, LANES), F32)] * groups
            for r in range(rows):
                here = row == r
                for g in range(groups):
                    got = jnp.take_along_axis(
                        cells[r, g * 8 : g * 8 + 8], lane, axis=1, mode="promise_in_bounds"
                    )
                    totals[g] = jnp.where(here, got, totals[g])
            for g in range(groups):
                send_buf[owner, g * 8 : g * 8 + 8, h * LANES : (h + 1) * LANES] = totals[g]

        @pl.when(j > 0)
        def _():
            profile_copy(owner).start()

        return 0

    lax.fori_loop(0, tiles, gather_owner, 0)
    own_copy = pltpu.make_async_copy(
        send_buf.at[t],
        prof_out.at[:, pl.ds(pl.multiple_of(t * cap, LANES), cap)],
        x_send.at[0],
    )
    own_copy.start()

    recv_round(qb, 1, 3, False)
    finish_backward(1, 3, store_adj)

    for k in range(levels):
        total = zero_plane
        for f in range(4):
            total = total + fin_out[f, k] * adj_out[f, k]
        runs[0, k] = total
    pairs = 8 // levels
    for r in range(rows // pairs):
        for k in range(levels):
            for h in range(pairs):
                at = r + h * (rows // pairs)
                sens_cells[r, k * pairs + h : k * pairs + h + 1] = runs[0, k, at : at + 1]

    sub_level = d * levels + sub // pairs
    sub_row = lax.rem(sub, pairs) * (rows // pairs)

    def gather_sens(owner, _):
        for h in range(halves):
            at = pl.ds(h * tiles + owner, 1)
            lane = jnp.broadcast_to(lane_tab[at, :], (8, LANES))
            row = jnp.broadcast_to(row_tab[at, :], (8, LANES)) - sub_row
            lev = jnp.broadcast_to(lev_tab[at, :], (8, LANES))
            first = lev >> 4
            kept = (sub_level >= first) & (sub_level <= first + (lev & 15))
            row = jnp.where(kept, row, -1)
            total = jnp.zeros((8, LANES), F32)
            for r in range(rows // pairs):
                got = jnp.take_along_axis(sens_cells[r], lane, axis=1, mode="promise_in_bounds")
                total = jnp.where(row == r, got, total)
            sens_part[at, :] = sens_scale * jnp.sum(total, axis=0, keepdims=True)
        return 0

    lax.fori_loop(0, tiles, gather_sens, 0)

    def sens_exchange(peer, slot):
        return remote(sens_part, sens_peer.at[slot], x_send.at[1 + peer], x_recv.at[slot], t, peer)

    def start_exchange(j, _):
        sens_exchange(lax.rem(d + j, depths), d).start()
        return 0

    def wait_exchange(j, total):
        peer = lax.rem(d + j, depths)
        sens_exchange(peer, peer).wait_recv()
        return total + sens_peer[peer]

    lax.fori_loop(1, depths, start_exchange, 0)
    total = lax.fori_loop(1, depths, wait_exchange, sens_part[...])
    for o in range(tiles):
        for h in range(halves):
            sens_send[o, :, h * LANES : (h + 1) * LANES] = total[h * tiles + o : h * tiles + o + 1]

    mine = pl.ds(pl.multiple_of(t * cap, LANES), cap)

    def sens_copy(owner):
        return remote(
            sens_send.at[owner], sens_out.at[:, mine], s_sem.at[0], s_sem.at[1], owner, d
        )

    def start_sens(j, _):
        sens_copy(lax.rem(t + j, tiles)).start()
        return 0

    lax.fori_loop(1, tiles, start_sens, 0)
    own_sens = pltpu.make_async_copy(sens_send.at[t], sens_out.at[:, mine], x_recv.at[d])
    own_sens.start()

    drain_round(qf, 0, 0, True)
    drain_round(qb, 0, 1, False)
    drain_round(qf, 1, 2, True)
    drain_round(qb, 1, 3, False)

    def drain_exchange(j, _):
        sens_exchange(lax.rem(d + j, depths), d).wait_send()
        return 0

    lax.fori_loop(1, depths, drain_exchange, 0)
    own_copy.wait()
    own_sens.wait()
    for buf, sems in ((send_buf, p_sem), (sens_send, s_sem)):
        all_but_one = buf.at[pl.ds(0, tiles - 1)]
        for way in range(2):
            pltpu.make_async_copy(all_but_one, all_but_one, sems.at[way]).wait()


def shards(
    perturbation,
    cotangent,
    land_mask,
    bottom_level,
    mix_gain,
    expansion,
    contraction,
    columns,
    owners,
    level_start,
    level_count,
):
    tiles, depths = lax.axis_size("tile"), lax.axis_size("depth")
    levels, rows, width = perturbation.shape[1:]
    cand = columns.shape[0]
    chunks = cand // LANES
    cap = 2 * cand // tiles
    planes = 4 * levels
    edge_rows = -(-(planes + levels) // 8) * 8

    def listed(x):
        return x.reshape(chunks, LANES)

    vmem = pl.BlockSpec(memory_space=pltpu.VMEM)
    hbm = pl.BlockSpec(memory_space=pl.ANY)
    state = (4, levels, rows, width)
    dma = pltpu.SemaphoreType.DMA
    final, adjoint, profiles, sensitivity = pl.pallas_call(
        functools.partial(kernel, tiles, depths),
        out_shape=(
            jax.ShapeDtypeStruct(state, F32),
            jax.ShapeDtypeStruct(state, F32),
            jax.ShapeDtypeStruct((planes, tiles * cap), F32),
            jax.ShapeDtypeStruct((1, tiles * cap), F32),
        ),
        in_specs=[vmem] * 11,
        out_specs=(vmem, vmem, hbm, hbm),
        scratch_shapes=[
            pltpu.VMEM((levels, rows, width), F32),
            pltpu.VMEM((levels, rows, width), F32),
            pltpu.VMEM((planes * rows, width), F32),
            pltpu.VMEM(state, F32),
            pltpu.VMEM(state, F32),
            pltpu.VMEM((2,) + state, F32),
            pltpu.VMEM((2, 4, levels + 2, rows, width), F32),
            pltpu.VMEM((2, 4, levels + 2, rows, width), F32),
            pltpu.VMEM((4, levels, rows, width), F32),
            pltpu.VMEM((4, 2, edge_rows, width), F32),
            pltpu.VMEM((4, 2, edge_rows, width), F32),
            pltpu.VMEM((4, rows, width), F32),
            pltpu.VMEM((4, depths, rows, width), F32),
            pltpu.VMEM((4, 2, 1, width), F32),
            pltpu.VMEM((4, 2, depths, 1, width), F32),
            pltpu.VMEM((chunks * tiles, 2 * LANES), BF16),
            pltpu.VMEM((chunks * tiles, LANES), F32),
            pltpu.VMEM((3 * tiles, cand), BF16),
            pltpu.VMEM((cap, cand), BF16),
            pltpu.VMEM((cap // LANES * tiles, LANES), I32),
            pltpu.VMEM((cap // LANES * tiles, LANES), I32),
            pltpu.VMEM((cap // LANES * tiles, LANES), I32),
            pltpu.VMEM((rows, planes, width), F32),
            pltpu.VMEM((rows * levels // 8, 8, width), F32),
            pltpu.VMEM((tiles, planes, cap), F32),
            pltpu.VMEM((cap // LANES * tiles, LANES), F32),
            pltpu.VMEM((depths, cap // LANES * tiles, LANES), F32),
            pltpu.VMEM((tiles, 1, cap), F32),
            dma((4, 2)),
            dma((4, 2)),
            dma((4, 2)),
            dma((4, 2)),
            dma((4, depths)),
            dma((4, depths)),
            dma((4, 2, depths)),
            dma((4, 2, depths)),
            dma((2,)),
            dma((2,)),
            dma((1 + depths,)),
            dma((depths,)),
        ],
        compiler_params=pltpu.CompilerParams(
            collective_id=0, has_side_effects=True, vmem_limit_bytes=32 * 1024 * 1024
        ),
    )(
        perturbation,
        cotangent,
        land_mask,
        bottom_level,
        mix_gain,
        expansion,
        contraction,
        listed(columns),
        listed(owners),
        listed(level_start),
        listed(level_count),
    )
    return final, adjoint, profiles.reshape(4, levels, 1, tiles * cap), sensitivity


def solution(mesh):
    placed = (
        P(None, "depth", "tile", None),
        P(None, "depth", "tile", None),
        P("tile", None),
        P("tile", None),
        P("depth", "tile", None),
        P("depth", "tile", None),
        P("depth", "tile", None),
        P("tile"),
        P("tile", None),
        P("tile"),
        P("tile"),
    )
    return jax.shard_map(
        shards,
        mesh=mesh,
        in_specs=placed,
        out_specs=(
            P(None, "depth", "tile", None),
            P(None, "depth", "tile", None),
            P(None, "depth", "tile", None),
            P("tile", None),
        ),
        check_vma=False,
    )
```

```python
import math

import jax
import jax.numpy as jnp
from jax import lax
from jax.experimental import pallas as pl
from jax.experimental.pallas import tpu as pltpu
from jax.sharding import PartitionSpec as P

STEPS = 2
LANES = 128
VMEM_BYTES = 60 * 1024 * 1024

nu_horiz = 0.06
nu_vert = 0.08
press_coef = 0.1
grav_step = 0.2
sens_scale = 0.2

MESH = pl.DeviceIdType.MESH
F32 = jnp.float32
BF16 = jnp.bfloat16
I32 = jnp.int32


def iota(shape, dim):
    return lax.broadcasted_iota(I32, shape, dim)


def lane_diff(p):
    return 0.5 * (pltpu.roll(p, p.shape[1] - 1, 1) - pltpu.roll(p, 1, 1))


def row_after(p, bottom):
    rows = p.shape[0]
    return jnp.where(iota(p.shape, 0) == rows - 1, bottom, pltpu.roll(p, rows - 1, 0))


def row_before(p, top):
    return jnp.where(iota(p.shape, 0) == 0, top, pltpu.roll(p, 1, 0))


def kernel(
    tiles,
    depths,
    inputs,
    fin_hbm,
    adj_hbm,
    prof_out,
    sens_out,
    held,
    fin_out,
    adj_out,
    out_sem,
    load_sem,
    wet,
    gw,
    fin,
    mid,
    amid,
    act,
    qf,
    qb,
    runs,
    edge_out,
    edge_in,
    tot_out,
    tot_in,
    diag_out,
    diag_in,
    rank_in,
    ranks,
    hot_own,
    hot_rank,
    lane_tab,
    row_tab,
    lev_tab,
    cells,
    sens_cells,
    send_buf,
    sens_part,
    sens_peer,
    sens_send,
    q_send,
    q_recv,
    e_send,
    e_recv,
    t_send,
    t_recv,
    d_send,
    d_recv,
    p_sem,
    s_sem,
    x_send,
    x_recv,
):
    pert, cot, land, bottom, gain, expan, contr, cols, owns, starts, counts = held
    loads = [pltpu.make_async_copy(a, b, load_sem.at[i]) for i, (a, b) in enumerate(zip(inputs, held))]
    for i in (2, 3, 4, 0, 5, 6, 1, 8, 7, 9, 10):
        loads[i].start()
    levels, rows = wet.shape[0], wet.shape[1]
    cap = hot_rank.shape[0]
    halves = cap // LANES
    chunks = owns.shape[0]
    planes = 4 * levels
    t = lax.axis_index("tile")
    d = lax.axis_index("depth")

    barrier = pltpu.get_barrier_semaphore()

    def greet(to_tile, to_depth):
        pl.semaphore_signal(barrier, inc=1, device_id=(to_tile, to_depth), device_id_type=MESH)

    def greet_depths(j, _):
        peer = lax.rem(d + j, depths)
        greet(t, peer)

        @pl.when(t > 0)
        def _():
            greet(t - 1, peer)

        @pl.when(t < tiles - 1)
        def _():
            greet(t + 1, peer)

        return 0

    lax.fori_loop(1, depths, greet_depths, 0)

    def greet_tiles(j, _):
        greet(lax.rem(t + j, tiles), d)
        return 0

    lax.fori_loop(1, tiles, greet_tiles, 0)

    zero_plane = jnp.zeros((rows, LANES), F32)
    for copy in loads:
        copy.wait()
    ocean = land[...] == 1
    for k in range(levels):
        w = jnp.where(ocean & (d * levels + k < bottom[...]), 1.0, 0.0).astype(F32)
        wet[k] = w
        gw[k] = w * gain[k]

    @pl.when(d == 0)
    def _():
        for s in range(2):
            for f in range(4):
                qf[s, f, 0] = zero_plane
                qb[s, f, 0] = zero_plane

    @pl.when(d == depths - 1)
    def _():
        for s in range(2):
            for f in range(4):
                qf[s, f, levels + 1] = zero_plane
                qb[s, f, levels + 1] = zero_plane

    def clear_side(side):
        for rnd in range(4):
            edge_in[rnd, side] = jnp.zeros(edge_in.shape[2:], F32)
            diag_in[rnd, side] = jnp.zeros(diag_in.shape[2:], F32)

    @pl.when(t == 0)
    def _():
        clear_side(0)

    @pl.when(t == tiles - 1)
    def _():
        clear_side(1)

    def store_edges(rnd, at, plane):
        edge_out[rnd, 0, at : at + 1] = plane[0:1]
        edge_out[rnd, 1, at : at + 1] = plane[rows - 1 : rows]

    def prepare_forward(src, s, rnd):
        running = zero_plane
        for k in range(levels):
            running = running + (contr[k] * src[1, k] - expan[k] * src[0, k])
            runs[rnd, k] = running
            store_edges(rnd, planes + k, running)
        tot_out[rnd] = running
        diag_out[rnd, 0] = running[0:1]
        diag_out[rnd, 1] = running[rows - 1 : rows]
        for f in range(4):
            for k in range(levels):
                q = gw[k] * src[f, k]
                qf[s, f, k + 1] = q
                store_edges(rnd, f * levels + k, q)

    def prepare_backward(src, s, rnd):
        run_u = zero_plane
        run_v = zero_plane
        zero_row = jnp.zeros((1, LANES), F32)
        for k in reversed(range(levels)):
            run_u = run_u + wet[k] * src[2, k]
            run_v = run_v + wet[k] * src[3, k]
            store_edges(rnd, planes + k, run_v)
            runs[rnd, k] = lane_diff(run_u) + 0.5 * (
                row_after(run_v, zero_row) - row_before(run_v, zero_row)
            )
        tot_out[rnd] = runs[rnd, 0]
        diag_out[rnd, 0] = run_v[0:1]
        diag_out[rnd, 1] = run_v[rows - 1 : rows]
        for f in range(4):
            for k in range(levels):
                a = wet[k] * src[f, k]
                act[s, f, k] = a
                q = gw[k] * a
                qb[s, f, k + 1] = q
                store_edges(rnd, f * levels + k, q)

    def remote(src, dst, send, recv, to_tile, to_depth):
        return pltpu.make_async_remote_copy(
            src_ref=src,
            dst_ref=dst,
            send_sem=send,
            recv_sem=recv,
            device_id=(to_tile, to_depth),
            device_id_type=MESH,
        )

    def level_up(q, s, rnd):
        return remote(
            q.at[s, :, levels], q.at[s, :, 0], q_send.at[rnd, 1], q_recv.at[rnd, 0], t, d + 1
        )

    def level_down(q, s, rnd):
        return remote(
            q.at[s, :, 1], q.at[s, :, levels + 1], q_send.at[rnd, 0], q_recv.at[rnd, 1], t, d - 1
        )

    def edge_copy(rnd, side):
        return remote(
            edge_out.at[rnd, side],
            edge_in.at[rnd, 1 - side],
            e_send.at[rnd, side],
            e_recv.at[rnd, 1 - side],
            t - 1 if side == 0 else t + 1,
            d,
        )

    def tot_copy(rnd, peer, slot):
        return remote(
            tot_out.at[rnd], tot_in.at[rnd, slot], t_send.at[rnd, peer], t_recv.at[rnd, slot], t, peer
        )

    def diag_copy(rnd, side, peer, slot):
        return remote(
            diag_out.at[rnd, side],
            diag_in.at[rnd, 1 - side, slot],
            d_send.at[rnd, side, peer],
            d_recv.at[rnd, 1 - side, slot],
            t - 1 if side == 0 else t + 1,
            peer,
        )

    has_side = (t > 0, t < tiles - 1)

    def ahead(forward):
        return (d + 1, depths) if forward else (0, d)

    def behind(forward):
        return (0, d) if forward else (d + 1, depths)

    def send_round(q, s, rnd, forward):
        @pl.when(d < depths - 1)
        def _():
            level_up(q, s, rnd).start()

        @pl.when(d > 0)
        def _():
            level_down(q, s, rnd).start()

        def one(peer, _):
            tot_copy(rnd, peer, d).start()
            for side in range(2):

                @pl.when(has_side[side])
                def _():
                    diag_copy(rnd, side, peer, d).start()

            return 0

        for side in range(2):

            @pl.when(has_side[side])
            def _():
                edge_copy(rnd, side).start()

        lax.fori_loop(*ahead(forward), one, 0)

    def recv_round(q, s, rnd, forward):
        def one(peer, _):
            tot_copy(rnd, peer, peer).wait_recv()
            for side in range(2):

                @pl.when(has_side[1 - side])
                def _():
                    diag_copy(rnd, side, peer, peer).wait_recv()

            return 0

        lax.fori_loop(*behind(forward), one, 0)
        for side in range(2):

            @pl.when(has_side[1 - side])
            def _():
                edge_copy(rnd, side).wait_recv()

        @pl.when(d > 0)
        def _():
            level_up(q, s, rnd).wait_recv()

        @pl.when(d < depths - 1)
        def _():
            level_down(q, s, rnd).wait_recv()

    def drain_round(q, s, rnd, forward):
        def one(peer, _):
            tot_copy(rnd, peer, d).wait_send()
            for side in range(2):

                @pl.when(has_side[side])
                def _():
                    diag_copy(rnd, side, peer, d).wait_send()

            return 0

        lax.fori_loop(*ahead(forward), one, 0)
        for side in range(2):

            @pl.when(has_side[side])
            def _():
                edge_copy(rnd, side).wait_send()

        @pl.when(d < depths - 1)
        def _():
            level_up(q, s, rnd).wait_send()

        @pl.when(d > 0)
        def _():
            level_down(q, s, rnd).wait_send()

    def base_sums(rnd, forward):
        def one(peer, carry):
            base, top, low = carry
            return (
                base + tot_in[rnd, peer],
                top + diag_in[rnd, 0, peer],
                low + diag_in[rnd, 1, peer],
            )

        zero_row = jnp.zeros((1, LANES), F32)
        return lax.fori_loop(*behind(forward), one, (zero_plane, zero_row, zero_row))

    def mixed(q, s, rnd, f, k):
        c = q[s, f, k + 1]
        at = f * levels + k
        north = row_after(c, edge_in[rnd, 1, at : at + 1])
        south = row_before(c, edge_in[rnd, 0, at : at + 1])
        horizontal = (
            north + south + pltpu.roll(c, 1, 1) + pltpu.roll(c, LANES - 1, 1) - 4.0 * c
        )
        vertical = q[s, f, k + 2] + q[s, f, k] - 2.0 * c
        return gw[k] * (nu_horiz * horizontal + nu_vert * vertical)

    row_ids = (t * rows + iota((rows, LANES), 0)).astype(F32)
    coriolis = 0.4 * jnp.sin(math.pi * ((row_ids + 0.5) / (tiles * rows) - 0.5))

    def finish_forward(src, s, rnd, store):
        base, top, low = base_sums(rnd, True)
        for k in range(levels):
            at = planes + k
            p = grav_step * (base + runs[rnd, k])
            p_top = grav_step * (top + edge_in[rnd, 0, at : at + 1])
            p_low = grav_step * (low + edge_in[rnd, 1, at : at + 1])
            gy = 0.5 * (row_after(p, p_low) - row_before(p, p_top))
            w = wet[k]
            for f in range(2):
                store(f, k, w * (src[f, k] + mixed(qf, s, rnd, f, k)))
            u, v = src[2, k], src[3, k]
            store(2, k, w * (u + mixed(qf, s, rnd, 2, k) + coriolis * v - press_coef * lane_diff(p)))
            store(3, k, w * (v + mixed(qf, s, rnd, 3, k) - coriolis * u - press_coef * gy))

    def finish_backward(s, rnd, store):
        base, top, low = base_sums(rnd, False)
        for k in range(levels):
            at = planes + k
            v_top = top + edge_in[rnd, 0, at : at + 1]
            v_low = low + edge_in[rnd, 1, at : at + 1]
            row = iota((rows, LANES), 0)
            rim = jnp.where(row == 0, -0.5 * v_top, 0.0) + jnp.where(row == rows - 1, 0.5 * v_low, 0.0)
            dens = (grav_step * press_coef) * (base + runs[rnd, k] + rim)
            a_t, a_s, a_u, a_v = (act[s, f, k] for f in range(4))
            store(0, k, a_t + mixed(qb, s, rnd, 0, k) - expan[k] * dens)
            store(1, k, a_s + mixed(qb, s, rnd, 1, k) + contr[k] * dens)
            store(2, k, a_u + mixed(qb, s, rnd, 2, k) - coriolis * a_v)
            store(3, k, a_v + mixed(qb, s, rnd, 3, k) + coriolis * a_u)

    prepare_forward(pert, 0, 0)
    prepare_backward(cot, 0, 1)

    sides = has_side[0].astype(I32) + has_side[1].astype(I32)
    pl.semaphore_wait(barrier, (depths - 1) * (1 + sides) + tiles - 1)

    send_round(qf, 0, 0, True)
    send_round(qb, 0, 1, False)

    own_ids = iota((tiles, LANES), 0)

    def rank_inputs(i, before):
        hot = (owns[pl.ds(i, 1), :] == own_ids).astype(F32)
        at = pl.multiple_of(i * tiles, tiles)
        rank_in[pl.ds(at, tiles), 0:LANES] = hot.astype(BF16)
        rank_in[pl.ds(at, tiles), LANES : 2 * LANES] = before.astype(BF16)
        return before + hot

    lax.fori_loop(0, chunks, rank_inputs, jnp.zeros((tiles, LANES), F32))
    i_row, i_col = iota((2 * LANES, LANES), 0), iota((2 * LANES, LANES), 1)
    earlier = jnp.where((i_row < i_col) | (i_row >= LANES), 1.0, 0.0).astype(BF16)
    ranks[...] = jnp.dot(rank_in[...], earlier, preferred_element_type=F32)
    slot_ids = iota((cap, LANES), 0)

    def slot_inputs(i, _):
        hot = (owns[pl.ds(i, 1), :] == own_ids).astype(F32)
        at = pl.multiple_of(i * tiles, tiles)
        lanes = pl.ds(pl.multiple_of(i * LANES, LANES), LANES)
        rank = jnp.sum(hot * ranks[pl.ds(at, tiles), :], axis=0, keepdims=True).astype(I32)
        hot_rank[:, lanes] = (slot_ids == rank).astype(F32).astype(BF16)
        c = cols[pl.ds(i, 1), :]
        lane = (c & (LANES - 1)).astype(F32)
        row = ((c >> 7) + 32).astype(F32)
        lev = (starts[pl.ds(i, 1), :] * 16 + counts[pl.ds(i, 1), :] - 1).astype(F32)
        hot_own[0:tiles, lanes] = (hot * lane).astype(BF16)
        hot_own[tiles : 2 * tiles, lanes] = (hot * row).astype(BF16)
        hot_own[2 * tiles : 3 * tiles, lanes] = (hot * lev).astype(BF16)
        return 0

    lax.fori_loop(0, chunks, slot_inputs, 0)
    table = lax.dot_general(
        hot_own[...], hot_rank[...], (((1,), (1,)), ((), ())), preferred_element_type=F32
    ).astype(I32)
    for h in range(halves):
        part = table[:, h * LANES : (h + 1) * LANES]
        lane_tab[h * tiles : (h + 1) * tiles] = part[0:tiles]
        row_tab[h * tiles : (h + 1) * tiles] = part[tiles : 2 * tiles] - 32
        lev_tab[h * tiles : (h + 1) * tiles] = part[2 * tiles : 3 * tiles]

    def store_mid(f, k, value):
        mid[f, k] = value

    def store_fin(f, k, value):
        fin_out[f, k] = value
        fin[(f * levels + k) * rows : (f * levels + k + 1) * rows] = value

    def store_amid(f, k, value):
        amid[f, k] = value

    def store_adj(f, k, value):
        adj_out[f, k] = value

    recv_round(qf, 0, 0, True)
    finish_forward(pert, 0, 0, store_mid)
    prepare_forward(mid, 1, 2)
    send_round(qf, 1, 2, True)
    recv_round(qb, 0, 1, False)
    finish_backward(0, 1, store_amid)
    prepare_backward(amid, 1, 3)
    send_round(qb, 1, 3, False)
    recv_round(qf, 1, 2, True)
    finish_forward(mid, 1, 2, store_fin)

    keep_fin = pltpu.make_async_copy(fin_out, fin_hbm, out_sem.at[0])
    keep_fin.start()

    groups = planes // 8
    for g in range(groups):
        for r in range(rows):
            cells[r, g * 8 : g * 8 + 8] = fin[pl.ds(g * 8 * rows + r, 8, stride=rows), :]

    sub = iota((8, LANES), 0)
    level_ids = d * levels + lax.rem(sub, levels)

    def profile_copy(owner):
        return remote(
            send_buf.at[owner],
            prof_out.at[:, pl.ds(pl.multiple_of(t * cap, LANES), cap)],
            p_sem.at[0],
            p_sem.at[1],
            owner,
            d,
        )

    def gather_owner(j, _):
        owner = lax.rem(t + j, tiles)
        for h in range(halves):
            at = pl.ds(h * tiles + owner, 1)
            lane = jnp.broadcast_to(lane_tab[at, :], (8, LANES))
            row = jnp.broadcast_to(row_tab[at, :], (8, LANES))
            lev = jnp.broadcast_to(lev_tab[at, :], (8, LANES))
            first = lev >> 4
            kept = (level_ids >= first) & (level_ids <= first + (lev & 15))
            row = jnp.where(kept, row, -1)
            totals = [jnp.zeros((8, LANES), F32)] * groups
            for r in range(rows):
                here = row == r
                for g in range(groups):
                    got = jnp.take_along_axis(
                        cells[r, g * 8 : g * 8 + 8], lane, axis=1, mode="promise_in_bounds"
                    )
                    totals[g] = jnp.where(here, got, totals[g])
            for g in range(groups):
                send_buf[owner, g * 8 : g * 8 + 8, h * LANES : (h + 1) * LANES] = totals[g]

        @pl.when(j > 0)
        def _():
            profile_copy(owner).start()

        return 0

    lax.fori_loop(0, tiles, gather_owner, 0)
    own_copy = pltpu.make_async_copy(
        send_buf.at[t],
        prof_out.at[:, pl.ds(pl.multiple_of(t * cap, LANES), cap)],
        x_send.at[0],
    )
    own_copy.start()

    recv_round(qb, 1, 3, False)
    finish_backward(1, 3, store_adj)

    keep_adj = pltpu.make_async_copy(adj_out, adj_hbm, out_sem.at[1])
    keep_adj.start()

    for k in range(levels):
        total = zero_plane
        for f in range(4):
            total = total + fin_out[f, k] * adj_out[f, k]
        runs[0, k] = total
    pairs = 8 // levels
    for r in range(rows // pairs):
        for k in range(levels):
            for h in range(pairs):
                at = r + h * (rows // pairs)
                sens_cells[r, k * pairs + h : k * pairs + h + 1] = runs[0, k, at : at + 1]

    sub_level = d * levels + sub // pairs
    sub_row = lax.rem(sub, pairs) * (rows // pairs)

    def gather_sens(owner, _):
        for h in range(halves):
            at = pl.ds(h * tiles + owner, 1)
            lane = jnp.broadcast_to(lane_tab[at, :], (8, LANES))
            row = jnp.broadcast_to(row_tab[at, :], (8, LANES)) - sub_row
            lev = jnp.broadcast_to(lev_tab[at, :], (8, LANES))
            first = lev >> 4
            kept = (sub_level >= first) & (sub_level <= first + (lev & 15))
            row = jnp.where(kept, row, -1)
            total = jnp.zeros((8, LANES), F32)
            for r in range(rows // pairs):
                got = jnp.take_along_axis(sens_cells[r], lane, axis=1, mode="promise_in_bounds")
                total = jnp.where(row == r, got, total)
            sens_part[at, :] = sens_scale * jnp.sum(total, axis=0, keepdims=True)
        return 0

    lax.fori_loop(0, tiles, gather_sens, 0)

    def sens_exchange(peer, slot):
        return remote(sens_part, sens_peer.at[slot], x_send.at[1 + peer], x_recv.at[slot], t, peer)

    def start_exchange(j, _):
        sens_exchange(lax.rem(d + j, depths), d).start()
        return 0

    def wait_exchange(j, total):
        peer = lax.rem(d + j, depths)
        sens_exchange(peer, peer).wait_recv()
        return total + sens_peer[peer]

    lax.fori_loop(1, depths, start_exchange, 0)
    total = lax.fori_loop(1, depths, wait_exchange, sens_part[...])
    for o in range(tiles):
        for h in range(halves):
            sens_send[o, :, h * LANES : (h + 1) * LANES] = total[h * tiles + o : h * tiles + o + 1]

    mine = pl.ds(pl.multiple_of(t * cap, LANES), cap)

    def sens_copy(owner):
        return remote(
            sens_send.at[owner], sens_out.at[:, mine], s_sem.at[0], s_sem.at[1], owner, d
        )

    def start_sens(j, _):
        sens_copy(lax.rem(t + j, tiles)).start()
        return 0

    lax.fori_loop(1, tiles, start_sens, 0)
    own_sens = pltpu.make_async_copy(sens_send.at[t], sens_out.at[:, mine], x_recv.at[d])
    own_sens.start()

    drain_round(qf, 0, 0, True)
    drain_round(qb, 0, 1, False)
    drain_round(qf, 1, 2, True)
    drain_round(qb, 1, 3, False)

    def drain_exchange(j, _):
        sens_exchange(lax.rem(d + j, depths), d).wait_send()
        return 0

    lax.fori_loop(1, depths, drain_exchange, 0)
    keep_fin.wait()
    keep_adj.wait()
    own_copy.wait()
    own_sens.wait()
    for buf, sems in ((send_buf, p_sem), (sens_send, s_sem)):
        all_but_one = buf.at[pl.ds(0, tiles - 1)]
        for way in range(2):
            pltpu.make_async_copy(all_but_one, all_but_one, sems.at[way]).wait()


def place(fin, adj, sens, prof, fin_out, adj_out, sens_out, prof_out, tiled, lined, sems):
    planes, width = prof.shape
    slots = width // LANES
    groups = planes // 8

    def copy(i, src, dst):
        made = pltpu.make_async_copy(src, dst, sems.at[i])
        made.start()
        return made

    tiles_of = [pl.ds(g * 8, 8) for g in range(groups)]
    loads = [copy(3 + g, prof.at[at], tiled.at[at]) for g, at in enumerate(tiles_of)]
    stores = [copy(0, fin, fin_out), copy(1, adj, adj_out), copy(2, sens, sens_out)]
    for g in range(groups):
        loads[g].wait()
        for at in range(slots):
            lined[pl.ds(g * 8 * slots + at, 8, stride=slots), :] = tiled[
                g * 8 : g * 8 + 8, at * LANES : (at + 1) * LANES
            ]
        part = pl.ds(g * 8 * slots, 8 * slots)
        stores.append(copy(3 + groups + g, lined.at[part], prof_out.at[part]))
    for made in stores:
        made.wait()


def shards(
    perturbation,
    cotangent,
    land_mask,
    bottom_level,
    mix_gain,
    expansion,
    contraction,
    columns,
    owners,
    level_start,
    level_count,
):
    tiles, depths = lax.axis_size("tile"), lax.axis_size("depth")
    levels, rows, width = perturbation.shape[1:]
    cand = columns.shape[0]
    chunks = cand // LANES
    cap = 2 * cand // tiles
    planes = 4 * levels
    edge_rows = -(-(planes + levels) // 8) * 8

    def listed(x):
        return x.reshape(chunks, LANES)

    slots = tiles * cap // LANES
    operands = (
        perturbation,
        cotangent,
        land_mask,
        bottom_level,
        mix_gain,
        expansion,
        contraction,
        listed(columns),
        listed(owners),
        listed(level_start),
        listed(level_count),
    )
    hbm = pl.BlockSpec(memory_space=pltpu.HBM)
    state = (4, levels, rows, width)
    dma = pltpu.SemaphoreType.DMA
    final, adjoint, profiles, sensitivity = pl.pallas_call(
        lambda *refs: kernel(
            tiles, depths, refs[:11], *refs[11:15], refs[18:29], *refs[15:18], *refs[29:]
        ),
        out_shape=(
            jax.ShapeDtypeStruct(state, F32),
            jax.ShapeDtypeStruct(state, F32),
            jax.ShapeDtypeStruct((planes, tiles * cap), F32),
            jax.ShapeDtypeStruct((1, tiles * cap), F32),
        ),
        in_specs=[hbm] * 11,
        out_specs=(hbm,) * 4,
        scratch_shapes=[
            pltpu.VMEM(state, F32),
            pltpu.VMEM(state, F32),
            dma((2,)),
            *[pltpu.VMEM(x.shape, x.dtype) for x in operands],
            dma((11,)),
            pltpu.VMEM((levels, rows, width), F32),
            pltpu.VMEM((levels, rows, width), F32),
            pltpu.VMEM((planes * rows, width), F32),
            pltpu.VMEM(state, F32),
            pltpu.VMEM(state, F32),
            pltpu.VMEM((2,) + state, F32),
            pltpu.VMEM((2, 4, levels + 2, rows, width), F32),
            pltpu.VMEM((2, 4, levels + 2, rows, width), F32),
            pltpu.VMEM((4, levels, rows, width), F32),
            pltpu.VMEM((4, 2, edge_rows, width), F32),
            pltpu.VMEM((4, 2, edge_rows, width), F32),
            pltpu.VMEM((4, rows, width), F32),
            pltpu.VMEM((4, depths, rows, width), F32),
            pltpu.VMEM((4, 2, 1, width), F32),
            pltpu.VMEM((4, 2, depths, 1, width), F32),
            pltpu.VMEM((chunks * tiles, 2 * LANES), BF16),
            pltpu.VMEM((chunks * tiles, LANES), F32),
            pltpu.VMEM((3 * tiles, cand), BF16),
            pltpu.VMEM((cap, cand), BF16),
            pltpu.VMEM((cap // LANES * tiles, LANES), I32),
            pltpu.VMEM((cap // LANES * tiles, LANES), I32),
            pltpu.VMEM((cap // LANES * tiles, LANES), I32),
            pltpu.VMEM((rows, planes, width), F32),
            pltpu.VMEM((rows * levels // 8, 8, width), F32),
            pltpu.VMEM((tiles, planes, cap), F32),
            pltpu.VMEM((cap // LANES * tiles, LANES), F32),
            pltpu.VMEM((depths, cap // LANES * tiles, LANES), F32),
            pltpu.VMEM((tiles, 1, cap), F32),
            dma((4, 2)),
            dma((4, 2)),
            dma((4, 2)),
            dma((4, 2)),
            dma((4, depths)),
            dma((4, depths)),
            dma((4, 2, depths)),
            dma((4, 2, depths)),
            dma((2,)),
            dma((2,)),
            dma((1 + depths,)),
            dma((depths,)),
        ],
        compiler_params=pltpu.CompilerParams(
            collective_id=0, has_side_effects=True, vmem_limit_bytes=VMEM_BYTES
        ),
    )(*operands)
    final, adjoint, sensitivity, profiles = pl.pallas_call(
        place,
        out_shape=(
            jax.ShapeDtypeStruct(state, F32),
            jax.ShapeDtypeStruct(state, F32),
            jax.ShapeDtypeStruct((1, tiles * cap), F32),
            jax.ShapeDtypeStruct((planes * slots, LANES), F32),
        ),
        in_specs=[hbm] * 4,
        out_specs=(hbm,) * 4,
        scratch_shapes=[
            pltpu.VMEM((planes, tiles * cap), F32),
            pltpu.VMEM((planes * slots, LANES), F32),
            dma((3 + planes // 4,)),
        ],
        compiler_params=pltpu.CompilerParams(vmem_limit_bytes=VMEM_BYTES),
    )(final, adjoint, sensitivity, profiles)
    return final, adjoint, profiles.reshape(4, levels, 1, tiles * cap), sensitivity


def solution(mesh):
    placed = (
        P(None, "depth", "tile", None),
        P(None, "depth", "tile", None),
        P("tile", None),
        P("tile", None),
        P("depth", "tile", None),
        P("depth", "tile", None),
        P("depth", "tile", None),
        P("tile"),
        P("tile", None),
        P("tile"),
        P("tile"),
    )
    return jax.shard_map(
        shards,
        mesh=mesh,
        in_specs=placed,
        out_specs=(
            P(None, "depth", "tile", None),
            P(None, "depth", "tile", None),
            P(None, "depth", "tile", None),
            P("tile", None),
        ),
        check_vma=False,
    )
```

```python
import math

import jax
import jax.numpy as jnp
from jax import lax
from jax.experimental import pallas as pl
from jax.experimental.pallas import tpu as pltpu
from jax.sharding import PartitionSpec as P

STEPS = 2
LANES = 128
VMEM_BYTES = 60 * 1024 * 1024

nu_horiz = 0.06
nu_vert = 0.08
press_coef = 0.1
grav_step = 0.2
sens_scale = 0.2

MESH = pl.DeviceIdType.MESH
F32 = jnp.float32
BF16 = jnp.bfloat16
I32 = jnp.int32


def iota(shape, dim):
    return lax.broadcasted_iota(I32, shape, dim)


def lane_diff(p):
    return 0.5 * (pltpu.roll(p, p.shape[1] - 1, 1) - pltpu.roll(p, 1, 1))


def row_after(p, bottom):
    rows = p.shape[0]
    return jnp.where(iota(p.shape, 0) == rows - 1, bottom, pltpu.roll(p, rows - 1, 0))


def row_before(p, top):
    return jnp.where(iota(p.shape, 0) == 0, top, pltpu.roll(p, 1, 0))


def kernel(
    tiles,
    depths,
    inputs,
    fin_hbm,
    adj_hbm,
    prof_out,
    sens_out,
    held,
    fin_out,
    adj_out,
    out_sem,
    load_sem,
    wet,
    gw,
    fin,
    mid,
    amid,
    act,
    qf,
    qb,
    runs,
    edge_out,
    edge_in,
    tot_out,
    tot_in,
    diag_out,
    diag_in,
    rank_in,
    ranks,
    hot_own,
    hot_rank,
    lane_tab,
    row_tab,
    lev_tab,
    cells,
    sens_cells,
    send_buf,
    sens_part,
    sens_peer,
    sens_send,
    q_send,
    q_recv,
    e_send,
    e_recv,
    t_send,
    t_recv,
    d_send,
    d_recv,
    p_sem,
    s_sem,
    x_send,
    x_recv,
):
    pert, cot, land, bottom, gain, expan, contr, cols, owns, starts, counts = held
    loads = [pltpu.make_async_copy(a, b, load_sem.at[i]) for i, (a, b) in enumerate(zip(inputs, held))]
    for i in (2, 3, 4, 0, 5, 6, 1, 8, 7, 9, 10):
        loads[i].start()
    levels, rows = wet.shape[0], wet.shape[1]
    cap = hot_rank.shape[0]
    halves = cap // LANES
    chunks = owns.shape[0]
    planes = 4 * levels
    t = lax.axis_index("tile")
    d = lax.axis_index("depth")

    barrier = pltpu.get_barrier_semaphore()

    def greet(to_tile, to_depth):
        pl.semaphore_signal(barrier, inc=1, device_id=(to_tile, to_depth), device_id_type=MESH)

    def greet_depths(j, _):
        peer = lax.rem(d + j, depths)
        greet(t, peer)

        @pl.when(t > 0)
        def _():
            greet(t - 1, peer)

        @pl.when(t < tiles - 1)
        def _():
            greet(t + 1, peer)

        return 0

    lax.fori_loop(1, depths, greet_depths, 0)

    def greet_tiles(j, _):
        greet(lax.rem(t + j, tiles), d)
        return 0

    lax.fori_loop(1, tiles, greet_tiles, 0)

    zero_plane = jnp.zeros((rows, LANES), F32)
    for copy in loads:
        copy.wait()
    ocean = land[...] == 1
    for k in range(levels):
        w = jnp.where(ocean & (d * levels + k < bottom[...]), 1.0, 0.0).astype(F32)
        wet[k] = w
        gw[k] = w * gain[k]

    @pl.when(d == 0)
    def _():
        for s in range(2):
            for f in range(4):
                qf[s, f, 0] = zero_plane
                qb[s, f, 0] = zero_plane

    @pl.when(d == depths - 1)
    def _():
        for s in range(2):
            for f in range(4):
                qf[s, f, levels + 1] = zero_plane
                qb[s, f, levels + 1] = zero_plane

    def clear_side(side):
        for rnd in range(4):
            edge_in[rnd, side] = jnp.zeros(edge_in.shape[2:], F32)
            diag_in[rnd, side] = jnp.zeros(diag_in.shape[2:], F32)

    @pl.when(t == 0)
    def _():
        clear_side(0)

    @pl.when(t == tiles - 1)
    def _():
        clear_side(1)

    def store_edges(rnd, at, plane):
        edge_out[rnd, 0, at : at + 1] = plane[0:1]
        edge_out[rnd, 1, at : at + 1] = plane[rows - 1 : rows]

    def prepare_forward(src, s, rnd):
        running = zero_plane
        for k in range(levels):
            running = running + (contr[k] * src[1, k] - expan[k] * src[0, k])
            runs[rnd, k] = running
            store_edges(rnd, planes + k, running)
        tot_out[rnd] = running
        diag_out[rnd, 0] = running[0:1]
        diag_out[rnd, 1] = running[rows - 1 : rows]
        for f in range(4):
            for k in range(levels):
                q = gw[k] * src[f, k]
                qf[s, f, k + 1] = q
                store_edges(rnd, f * levels + k, q)

    def prepare_backward(src, s, rnd):
        run_u = zero_plane
        run_v = zero_plane
        zero_row = jnp.zeros((1, LANES), F32)
        for k in reversed(range(levels)):
            run_u = run_u + wet[k] * src[2, k]
            run_v = run_v + wet[k] * src[3, k]
            store_edges(rnd, planes + k, run_v)
            runs[rnd, k] = lane_diff(run_u) + 0.5 * (
                row_after(run_v, zero_row) - row_before(run_v, zero_row)
            )
        tot_out[rnd] = runs[rnd, 0]
        diag_out[rnd, 0] = run_v[0:1]
        diag_out[rnd, 1] = run_v[rows - 1 : rows]
        for f in range(4):
            for k in range(levels):
                a = wet[k] * src[f, k]
                act[s, f, k] = a
                q = gw[k] * a
                qb[s, f, k + 1] = q
                store_edges(rnd, f * levels + k, q)

    def remote(src, dst, send, recv, to_tile, to_depth):
        return pltpu.make_async_remote_copy(
            src_ref=src,
            dst_ref=dst,
            send_sem=send,
            recv_sem=recv,
            device_id=(to_tile, to_depth),
            device_id_type=MESH,
        )

    def level_up(q, s, rnd):
        return remote(
            q.at[s, :, levels], q.at[s, :, 0], q_send.at[rnd, 1], q_recv.at[rnd, 0], t, d + 1
        )

    def level_down(q, s, rnd):
        return remote(
            q.at[s, :, 1], q.at[s, :, levels + 1], q_send.at[rnd, 0], q_recv.at[rnd, 1], t, d - 1
        )

    def edge_copy(rnd, side):
        return remote(
            edge_out.at[rnd, side],
            edge_in.at[rnd, 1 - side],
            e_send.at[rnd, side],
            e_recv.at[rnd, 1 - side],
            t - 1 if side == 0 else t + 1,
            d,
        )

    def tot_copy(rnd, peer, slot):
        return remote(
            tot_out.at[rnd], tot_in.at[rnd, slot], t_send.at[rnd, peer], t_recv.at[rnd, slot], t, peer
        )

    def diag_copy(rnd, side, peer, slot):
        return remote(
            diag_out.at[rnd, side],
            diag_in.at[rnd, 1 - side, slot],
            d_send.at[rnd, side, peer],
            d_recv.at[rnd, 1 - side, slot],
            t - 1 if side == 0 else t + 1,
            peer,
        )

    has_side = (t > 0, t < tiles - 1)

    def ahead(forward):
        return (d + 1, depths) if forward else (0, d)

    def behind(forward):
        return (0, d) if forward else (d + 1, depths)

    def send_round(q, s, rnd, forward):
        @pl.when(d < depths - 1)
        def _():
            level_up(q, s, rnd).start()

        @pl.when(d > 0)
        def _():
            level_down(q, s, rnd).start()

        def one(peer, _):
            tot_copy(rnd, peer, d).start()
            for side in range(2):

                @pl.when(has_side[side])
                def _():
                    diag_copy(rnd, side, peer, d).start()

            return 0

        for side in range(2):

            @pl.when(has_side[side])
            def _():
                edge_copy(rnd, side).start()

        lax.fori_loop(*ahead(forward), one, 0)

    def recv_round(q, s, rnd, forward):
        def one(peer, _):
            tot_copy(rnd, peer, peer).wait_recv()
            for side in range(2):

                @pl.when(has_side[1 - side])
                def _():
                    diag_copy(rnd, side, peer, peer).wait_recv()

            return 0

        lax.fori_loop(*behind(forward), one, 0)
        for side in range(2):

            @pl.when(has_side[1 - side])
            def _():
                edge_copy(rnd, side).wait_recv()

        @pl.when(d > 0)
        def _():
            level_up(q, s, rnd).wait_recv()

        @pl.when(d < depths - 1)
        def _():
            level_down(q, s, rnd).wait_recv()

    def drain_round(q, s, rnd, forward):
        def one(peer, _):
            tot_copy(rnd, peer, d).wait_send()
            for side in range(2):

                @pl.when(has_side[side])
                def _():
                    diag_copy(rnd, side, peer, d).wait_send()

            return 0

        lax.fori_loop(*ahead(forward), one, 0)
        for side in range(2):

            @pl.when(has_side[side])
            def _():
                edge_copy(rnd, side).wait_send()

        @pl.when(d < depths - 1)
        def _():
            level_up(q, s, rnd).wait_send()

        @pl.when(d > 0)
        def _():
            level_down(q, s, rnd).wait_send()

    def base_sums(rnd, forward):
        def one(peer, carry):
            base, top, low = carry
            return (
                base + tot_in[rnd, peer],
                top + diag_in[rnd, 0, peer],
                low + diag_in[rnd, 1, peer],
            )

        zero_row = jnp.zeros((1, LANES), F32)
        return lax.fori_loop(*behind(forward), one, (zero_plane, zero_row, zero_row))

    def mixed(q, s, rnd, f, k):
        c = q[s, f, k + 1]
        at = f * levels + k
        north = row_after(c, edge_in[rnd, 1, at : at + 1])
        south = row_before(c, edge_in[rnd, 0, at : at + 1])
        horizontal = (
            north + south + pltpu.roll(c, 1, 1) + pltpu.roll(c, LANES - 1, 1) - 4.0 * c
        )
        vertical = q[s, f, k + 2] + q[s, f, k] - 2.0 * c
        return gw[k] * (nu_horiz * horizontal + nu_vert * vertical)

    row_ids = (t * rows + iota((rows, LANES), 0)).astype(F32)
    coriolis = 0.4 * jnp.sin(math.pi * ((row_ids + 0.5) / (tiles * rows) - 0.5))

    def finish_forward(src, s, rnd, store):
        base, top, low = base_sums(rnd, True)
        for k in range(levels):
            at = planes + k
            p = grav_step * (base + runs[rnd, k])
            p_top = grav_step * (top + edge_in[rnd, 0, at : at + 1])
            p_low = grav_step * (low + edge_in[rnd, 1, at : at + 1])
            gy = 0.5 * (row_after(p, p_low) - row_before(p, p_top))
            w = wet[k]
            for f in range(2):
                store(f, k, w * (src[f, k] + mixed(qf, s, rnd, f, k)))
            u, v = src[2, k], src[3, k]
            store(2, k, w * (u + mixed(qf, s, rnd, 2, k) + coriolis * v - press_coef * lane_diff(p)))
            store(3, k, w * (v + mixed(qf, s, rnd, 3, k) - coriolis * u - press_coef * gy))

    def finish_backward(s, rnd, store):
        base, top, low = base_sums(rnd, False)
        for k in range(levels):
            at = planes + k
            v_top = top + edge_in[rnd, 0, at : at + 1]
            v_low = low + edge_in[rnd, 1, at : at + 1]
            row = iota((rows, LANES), 0)
            rim = jnp.where(row == 0, -0.5 * v_top, 0.0) + jnp.where(row == rows - 1, 0.5 * v_low, 0.0)
            dens = (grav_step * press_coef) * (base + runs[rnd, k] + rim)
            a_t, a_s, a_u, a_v = (act[s, f, k] for f in range(4))
            store(0, k, a_t + mixed(qb, s, rnd, 0, k) - expan[k] * dens)
            store(1, k, a_s + mixed(qb, s, rnd, 1, k) + contr[k] * dens)
            store(2, k, a_u + mixed(qb, s, rnd, 2, k) - coriolis * a_v)
            store(3, k, a_v + mixed(qb, s, rnd, 3, k) + coriolis * a_u)

    prepare_forward(pert, 0, 0)
    prepare_backward(cot, 0, 1)

    sides = has_side[0].astype(I32) + has_side[1].astype(I32)
    pl.semaphore_wait(barrier, (depths - 1) * (1 + sides) + tiles - 1)

    send_round(qf, 0, 0, True)
    send_round(qb, 0, 1, False)

    own_ids = iota((tiles, LANES), 0)

    def rank_inputs(i, before):
        hot = (owns[pl.ds(i, 1), :] == own_ids).astype(F32)
        at = pl.multiple_of(i * tiles, tiles)
        rank_in[pl.ds(at, tiles), 0:LANES] = hot.astype(BF16)
        rank_in[pl.ds(at, tiles), LANES : 2 * LANES] = before.astype(BF16)
        return before + hot

    lax.fori_loop(0, chunks, rank_inputs, jnp.zeros((tiles, LANES), F32))
    i_row, i_col = iota((2 * LANES, LANES), 0), iota((2 * LANES, LANES), 1)
    earlier = jnp.where((i_row < i_col) | (i_row >= LANES), 1.0, 0.0).astype(BF16)
    ranks[...] = jnp.dot(rank_in[...], earlier, preferred_element_type=F32)
    slot_ids = iota((cap, LANES), 0)

    def slot_inputs(i, _):
        hot = (owns[pl.ds(i, 1), :] == own_ids).astype(F32)
        at = pl.multiple_of(i * tiles, tiles)
        lanes = pl.ds(pl.multiple_of(i * LANES, LANES), LANES)
        rank = jnp.sum(hot * ranks[pl.ds(at, tiles), :], axis=0, keepdims=True).astype(I32)
        hot_rank[:, lanes] = (slot_ids == rank).astype(F32).astype(BF16)
        c = cols[pl.ds(i, 1), :]
        lane = (c & (LANES - 1)).astype(F32)
        row = ((c >> 7) + 32).astype(F32)
        lev = (starts[pl.ds(i, 1), :] * 16 + counts[pl.ds(i, 1), :] - 1).astype(F32)
        hot_own[0:tiles, lanes] = (hot * lane).astype(BF16)
        hot_own[tiles : 2 * tiles, lanes] = (hot * row).astype(BF16)
        hot_own[2 * tiles : 3 * tiles, lanes] = (hot * lev).astype(BF16)
        return 0

    lax.fori_loop(0, chunks, slot_inputs, 0)
    table = lax.dot_general(
        hot_own[...], hot_rank[...], (((1,), (1,)), ((), ())), preferred_element_type=F32
    ).astype(I32)
    for h in range(halves):
        part = table[:, h * LANES : (h + 1) * LANES]
        lane_tab[h * tiles : (h + 1) * tiles] = part[0:tiles]
        row_tab[h * tiles : (h + 1) * tiles] = part[tiles : 2 * tiles] - 32
        lev_tab[h * tiles : (h + 1) * tiles] = part[2 * tiles : 3 * tiles]

    def store_mid(f, k, value):
        mid[f, k] = value

    def store_fin(f, k, value):
        fin_out[f, k] = value
        fin[(f * levels + k) * rows : (f * levels + k + 1) * rows] = value

    def store_amid(f, k, value):
        amid[f, k] = value

    def store_adj(f, k, value):
        adj_out[f, k] = value

    recv_round(qf, 0, 0, True)
    finish_forward(pert, 0, 0, store_mid)
    prepare_forward(mid, 1, 2)
    send_round(qf, 1, 2, True)
    recv_round(qb, 0, 1, False)
    finish_backward(0, 1, store_amid)
    prepare_backward(amid, 1, 3)
    send_round(qb, 1, 3, False)
    recv_round(qf, 1, 2, True)
    finish_forward(mid, 1, 2, store_fin)

    keep_fin = pltpu.make_async_copy(fin_out, fin_hbm, out_sem.at[0])
    keep_fin.start()

    groups = planes // 8
    for g in range(groups):
        for r in range(rows):
            cells[r, g * 8 : g * 8 + 8] = fin[pl.ds(g * 8 * rows + r, 8, stride=rows), :]

    sub = iota((8, LANES), 0)
    level_ids = d * levels + lax.rem(sub, levels)

    def profile_copy(owner):
        return remote(
            send_buf.at[owner],
            prof_out.at[:, pl.ds(pl.multiple_of(t * cap, LANES), cap)],
            p_sem.at[0],
            p_sem.at[1],
            owner,
            d,
        )

    def gather_owner(j, _):
        owner = lax.rem(t + j, tiles)
        for h in range(halves):
            at = pl.ds(h * tiles + owner, 1)
            lane = jnp.broadcast_to(lane_tab[at, :], (8, LANES))
            row = jnp.broadcast_to(row_tab[at, :], (8, LANES))
            lev = jnp.broadcast_to(lev_tab[at, :], (8, LANES))
            first = lev >> 4
            kept = (level_ids >= first) & (level_ids <= first + (lev & 15))
            row = jnp.where(kept, row, -1)
            totals = [jnp.zeros((8, LANES), F32)] * groups
            for r in range(rows):
                here = row == r
                for g in range(groups):
                    got = jnp.take_along_axis(
                        cells[r, g * 8 : g * 8 + 8], lane, axis=1, mode="promise_in_bounds"
                    )
                    totals[g] = jnp.where(here, got, totals[g])
            for g in range(groups):
                send_buf[owner, g * 8 : g * 8 + 8, h * LANES : (h + 1) * LANES] = totals[g]

        @pl.when(j < tiles)
        def _():
            profile_copy(owner).start()

        return 0

    first_part, second_part = 1 + tiles * 8 // 32, 1 + tiles * 31 // 32
    lax.fori_loop(1, first_part, gather_owner, 0)
    recv_round(qb, 1, 3, False)
    finish_backward(1, 3, store_adj)

    keep_adj = pltpu.make_async_copy(adj_out, adj_hbm, out_sem.at[1])
    keep_adj.start()

    for k in range(levels):
        total = zero_plane
        for f in range(4):
            total = total + fin_out[f, k] * adj_out[f, k]
        runs[0, k] = total
    pairs = 8 // levels
    for r in range(rows // pairs):
        for k in range(levels):
            for h in range(pairs):
                at = r + h * (rows // pairs)
                sens_cells[r, k * pairs + h : k * pairs + h + 1] = runs[0, k, at : at + 1]

    sub_level = d * levels + sub // pairs
    sub_row = lax.rem(sub, pairs) * (rows // pairs)

    def gather_sens(owner, _):
        for h in range(halves):
            at = pl.ds(h * tiles + owner, 1)
            lane = jnp.broadcast_to(lane_tab[at, :], (8, LANES))
            row = jnp.broadcast_to(row_tab[at, :], (8, LANES)) - sub_row
            lev = jnp.broadcast_to(lev_tab[at, :], (8, LANES))
            first = lev >> 4
            kept = (sub_level >= first) & (sub_level <= first + (lev & 15))
            row = jnp.where(kept, row, -1)
            total = jnp.zeros((8, LANES), F32)
            for r in range(rows // pairs):
                got = jnp.take_along_axis(sens_cells[r], lane, axis=1, mode="promise_in_bounds")
                total = jnp.where(row == r, got, total)
            sens_part[at, :] = sens_scale * jnp.sum(total, axis=0, keepdims=True)
        return 0

    lax.fori_loop(0, tiles, gather_sens, 0, unroll=4)

    def sens_exchange(peer, slot):
        return remote(sens_part, sens_peer.at[slot], x_send.at[1 + peer], x_recv.at[slot], t, peer)

    def start_exchange(j, _):
        sens_exchange(lax.rem(d + j, depths), d).start()
        return 0

    def wait_exchange(j, total):
        peer = lax.rem(d + j, depths)
        sens_exchange(peer, peer).wait_recv()
        return total + sens_peer[peer]

    lax.fori_loop(1, depths, start_exchange, 0)
    lax.fori_loop(first_part, second_part, gather_owner, 0)
    total = lax.fori_loop(1, depths, wait_exchange, sens_part[...])
    for o in range(tiles):
        for h in range(halves):
            sens_send[o, :, h * LANES : (h + 1) * LANES] = total[h * tiles + o : h * tiles + o + 1]

    mine = pl.ds(pl.multiple_of(t * cap, LANES), cap)

    def sens_copy(owner):
        return remote(
            sens_send.at[owner], sens_out.at[:, mine], s_sem.at[0], s_sem.at[1], owner, d
        )

    def start_sens(j, _):
        sens_copy(lax.rem(t + j, tiles)).start()
        return 0

    lax.fori_loop(1, tiles, start_sens, 0)
    own_sens = pltpu.make_async_copy(sens_send.at[t], sens_out.at[:, mine], x_recv.at[d])
    own_sens.start()
    lax.fori_loop(second_part, tiles + 1, gather_owner, 0)
    own_copy = pltpu.make_async_copy(
        send_buf.at[t],
        prof_out.at[:, pl.ds(pl.multiple_of(t * cap, LANES), cap)],
        x_send.at[0],
    )
    own_copy.start()


    drain_round(qf, 0, 0, True)
    drain_round(qb, 0, 1, False)
    drain_round(qf, 1, 2, True)
    drain_round(qb, 1, 3, False)

    def drain_exchange(j, _):
        sens_exchange(lax.rem(d + j, depths), d).wait_send()
        return 0

    lax.fori_loop(1, depths, drain_exchange, 0)
    keep_fin.wait()
    keep_adj.wait()
    own_copy.wait()
    own_sens.wait()
    for buf, sems in ((send_buf, p_sem), (sens_send, s_sem)):
        all_but_one = buf.at[pl.ds(0, tiles - 1)]
        for way in range(2):
            pltpu.make_async_copy(all_but_one, all_but_one, sems.at[way]).wait()


def place(fin, adj, sens, prof, fin_out, adj_out, sens_out, prof_out, *scratch):
    fin_held, adj_held, sens_held, tiled, lined, sems = scratch
    planes, width = prof.shape
    slots = width // LANES
    groups = planes // 8

    def copy(i, src, dst):
        made = pltpu.make_async_copy(src, dst, sems.at[i])
        made.start()
        return made

    loads = [
        copy(g, prof.at[pl.ds(g * 8, 8)], tiled.at[pl.ds(g * 8, 8)]) for g in range(groups)
    ]
    passed = ((fin, fin_held, fin_out), (adj, adj_held, adj_out), (sens, sens_held, sens_out))
    loads += [copy(groups + i, src, held) for i, (src, held, _) in enumerate(passed)]
    stores = []
    for i, (_, held, out) in enumerate(passed):
        loads[groups + i].wait()
        stores.append(copy(groups + 3 + i, held, out))
    for g in range(groups):
        loads[g].wait()
        for at in range(slots):
            lined[pl.ds(g * 8 * slots + at, 8, stride=slots), :] = tiled[
                g * 8 : g * 8 + 8, at * LANES : (at + 1) * LANES
            ]
        part = pl.ds(g * 8 * slots, 8 * slots)
        stores.append(copy(groups + 6 + g, lined.at[part], prof_out.at[part]))
    for made in stores:
        made.wait()


def shards(
    perturbation,
    cotangent,
    land_mask,
    bottom_level,
    mix_gain,
    expansion,
    contraction,
    columns,
    owners,
    level_start,
    level_count,
):
    tiles, depths = lax.axis_size("tile"), lax.axis_size("depth")
    levels, rows, width = perturbation.shape[1:]
    cand = columns.shape[0]
    chunks = cand // LANES
    cap = 2 * cand // tiles
    planes = 4 * levels
    edge_rows = -(-(planes + levels) // 8) * 8

    def listed(x):
        return x.reshape(chunks, LANES)

    slots = tiles * cap // LANES
    operands = (
        perturbation,
        cotangent,
        land_mask,
        bottom_level,
        mix_gain,
        expansion,
        contraction,
        listed(columns),
        listed(owners),
        listed(level_start),
        listed(level_count),
    )
    hbm = pl.BlockSpec(memory_space=pltpu.HBM)
    state = (4, levels, rows, width)
    dma = pltpu.SemaphoreType.DMA
    final, adjoint, profiles, sensitivity = pl.pallas_call(
        lambda *refs: kernel(
            tiles, depths, refs[:11], *refs[11:15], refs[18:29], *refs[15:18], *refs[29:]
        ),
        out_shape=(
            jax.ShapeDtypeStruct(state, F32),
            jax.ShapeDtypeStruct(state, F32),
            jax.ShapeDtypeStruct((planes, tiles * cap), F32),
            jax.ShapeDtypeStruct((1, tiles * cap), F32),
        ),
        in_specs=[hbm] * 11,
        out_specs=(hbm,) * 4,
        scratch_shapes=[
            pltpu.VMEM(state, F32),
            pltpu.VMEM(state, F32),
            dma((2,)),
            *[pltpu.VMEM(x.shape, x.dtype) for x in operands],
            dma((11,)),
            pltpu.VMEM((levels, rows, width), F32),
            pltpu.VMEM((levels, rows, width), F32),
            pltpu.VMEM((planes * rows, width), F32),
            pltpu.VMEM(state, F32),
            pltpu.VMEM(state, F32),
            pltpu.VMEM((2,) + state, F32),
            pltpu.VMEM((2, 4, levels + 2, rows, width), F32),
            pltpu.VMEM((2, 4, levels + 2, rows, width), F32),
            pltpu.VMEM((4, levels, rows, width), F32),
            pltpu.VMEM((4, 2, edge_rows, width), F32),
            pltpu.VMEM((4, 2, edge_rows, width), F32),
            pltpu.VMEM((4, rows, width), F32),
            pltpu.VMEM((4, depths, rows, width), F32),
            pltpu.VMEM((4, 2, 1, width), F32),
            pltpu.VMEM((4, 2, depths, 1, width), F32),
            pltpu.VMEM((chunks * tiles, 2 * LANES), BF16),
            pltpu.VMEM((chunks * tiles, LANES), F32),
            pltpu.VMEM((3 * tiles, cand), BF16),
            pltpu.VMEM((cap, cand), BF16),
            pltpu.VMEM((cap // LANES * tiles, LANES), I32),
            pltpu.VMEM((cap // LANES * tiles, LANES), I32),
            pltpu.VMEM((cap // LANES * tiles, LANES), I32),
            pltpu.VMEM((rows, planes, width), F32),
            pltpu.VMEM((rows * levels // 8, 8, width), F32),
            pltpu.VMEM((tiles, planes, cap), F32),
            pltpu.VMEM((cap // LANES * tiles, LANES), F32),
            pltpu.VMEM((depths, cap // LANES * tiles, LANES), F32),
            pltpu.VMEM((tiles, 1, cap), F32),
            dma((4, 2)),
            dma((4, 2)),
            dma((4, 2)),
            dma((4, 2)),
            dma((4, depths)),
            dma((4, depths)),
            dma((4, 2, depths)),
            dma((4, 2, depths)),
            dma((2,)),
            dma((2,)),
            dma((1 + depths,)),
            dma((depths,)),
        ],
        compiler_params=pltpu.CompilerParams(
            collective_id=0, has_side_effects=True, vmem_limit_bytes=VMEM_BYTES
        ),
    )(*operands)
    final, adjoint, sensitivity, profiles = pl.pallas_call(
        place,
        out_shape=(
            jax.ShapeDtypeStruct(state, F32),
            jax.ShapeDtypeStruct(state, F32),
            jax.ShapeDtypeStruct((1, tiles * cap), F32),
            jax.ShapeDtypeStruct((planes * slots, LANES), F32),
        ),
        in_specs=[hbm] * 4,
        out_specs=(hbm,) * 4,
        scratch_shapes=[
            pltpu.VMEM(state, F32),
            pltpu.VMEM(state, F32),
            pltpu.VMEM((1, tiles * cap), F32),
            pltpu.VMEM((planes, tiles * cap), F32),
            pltpu.VMEM((planes * slots, LANES), F32),
            dma((6 + planes // 4,)),
        ],
        compiler_params=pltpu.CompilerParams(vmem_limit_bytes=VMEM_BYTES),
    )(final, adjoint, sensitivity, profiles)
    return final, adjoint, profiles.reshape(4, levels, 1, tiles * cap), sensitivity


def solution(mesh):
    placed = (
        P(None, "depth", "tile", None),
        P(None, "depth", "tile", None),
        P("tile", None),
        P("tile", None),
        P("depth", "tile", None),
        P("depth", "tile", None),
        P("depth", "tile", None),
        P("tile"),
        P("tile", None),
        P("tile"),
        P("tile"),
    )
    return jax.shard_map(
        shards,
        mesh=mesh,
        in_specs=placed,
        out_specs=(
            P(None, "depth", "tile", None),
            P(None, "depth", "tile", None),
            P(None, "depth", "tile", None),
            P("tile", None),
        ),
        check_vma=False,
    )
```

```python
import math

import jax
import jax.numpy as jnp
from jax import lax
from jax.experimental import pallas as pl
from jax.experimental.pallas import tpu as pltpu
from jax.sharding import PartitionSpec as P

STEPS = 2
LANES = 128
VMEM_BYTES = 60 * 1024 * 1024

nu_horiz = 0.06
nu_vert = 0.08
press_coef = 0.1
grav_step = 0.2
sens_scale = 0.2

MESH = pl.DeviceIdType.MESH
F32 = jnp.float32
BF16 = jnp.bfloat16
I32 = jnp.int32


def iota(shape, dim):
    return lax.broadcasted_iota(I32, shape, dim)


def lane_diff(p):
    return 0.5 * (pltpu.roll(p, p.shape[1] - 1, 1) - pltpu.roll(p, 1, 1))


def row_after(p, bottom):
    rows = p.shape[0]
    return jnp.where(iota(p.shape, 0) == rows - 1, bottom, pltpu.roll(p, rows - 1, 0))


def row_before(p, top):
    return jnp.where(iota(p.shape, 0) == 0, top, pltpu.roll(p, 1, 0))


def kernel(
    tiles,
    depths,
    inputs,
    fin_hbm,
    adj_hbm,
    prof_out,
    sens_out,
    held,
    fin_out,
    adj_out,
    out_sem,
    load_sem,
    wet,
    gw,
    fin,
    mid,
    amid,
    act,
    qf,
    qb,
    runs,
    edge_out,
    edge_in,
    tot_out,
    tot_in,
    diag_out,
    diag_in,
    rank_in,
    ranks,
    hot_own,
    hot_rank,
    lane_tab,
    row_tab,
    lev_tab,
    cells,
    sens_cells,
    send_buf,
    sens_part,
    sens_peer,
    sens_send,
    q_send,
    q_recv,
    e_send,
    e_recv,
    t_send,
    t_recv,
    d_send,
    d_recv,
    p_sem,
    s_sem,
    x_send,
    x_recv,
):
    pert, cot, land, bottom, gain, expan, contr, cols, owns, starts, counts = held
    loads = [pltpu.make_async_copy(a, b, load_sem.at[i]) for i, (a, b) in enumerate(zip(inputs, held))]
    for i in (2, 3, 4, 0, 5, 6, 1, 8, 7, 9, 10):
        loads[i].start()
    levels, rows = wet.shape[0], wet.shape[1]
    cap = hot_rank.shape[0]
    halves = cap // LANES
    chunks = owns.shape[0]
    planes = 4 * levels
    t = lax.axis_index("tile")
    d = lax.axis_index("depth")

    barrier = pltpu.get_barrier_semaphore()

    def greet(to_tile, to_depth):
        pl.semaphore_signal(barrier, inc=1, device_id=(to_tile, to_depth), device_id_type=MESH)

    def greet_depths(j, _):
        peer = lax.rem(d + j, depths)
        greet(t, peer)

        @pl.when(t > 0)
        def _():
            greet(t - 1, peer)

        @pl.when(t < tiles - 1)
        def _():
            greet(t + 1, peer)

        return 0

    lax.fori_loop(1, depths, greet_depths, 0)

    def greet_tiles(j, _):
        greet(lax.rem(t + j, tiles), d)
        return 0

    lax.fori_loop(1, tiles, greet_tiles, 0)

    zero_plane = jnp.zeros((rows, LANES), F32)

    def loaded(*which):
        for i in which:
            loads[i].wait()

    loaded(2, 3, 4, 0, 5, 6)
    ocean = land[...] == 1
    for k in range(levels):
        w = jnp.where(ocean & (d * levels + k < bottom[...]), 1.0, 0.0).astype(F32)
        wet[k] = w
        gw[k] = w * gain[k]

    @pl.when(d == 0)
    def _():
        for s in range(2):
            for f in range(4):
                qf[s, f, 0] = zero_plane
                qb[s, f, 0] = zero_plane

    @pl.when(d == depths - 1)
    def _():
        for s in range(2):
            for f in range(4):
                qf[s, f, levels + 1] = zero_plane
                qb[s, f, levels + 1] = zero_plane

    def clear_side(side):
        for rnd in range(4):
            edge_in[rnd, side] = jnp.zeros(edge_in.shape[2:], F32)
            diag_in[rnd, side] = jnp.zeros(diag_in.shape[2:], F32)

    @pl.when(t == 0)
    def _():
        clear_side(0)

    @pl.when(t == tiles - 1)
    def _():
        clear_side(1)

    def store_edges(rnd, at, plane):
        edge_out[rnd, 0, at : at + 1] = plane[0:1]
        edge_out[rnd, 1, at : at + 1] = plane[rows - 1 : rows]

    def prepare_forward(src, s, rnd):
        running = zero_plane
        for k in range(levels):
            running = running + (contr[k] * src[1, k] - expan[k] * src[0, k])
            runs[rnd, k] = running
            store_edges(rnd, planes + k, running)
        tot_out[rnd] = running
        diag_out[rnd, 0] = running[0:1]
        diag_out[rnd, 1] = running[rows - 1 : rows]
        for f in range(4):
            for k in range(levels):
                q = gw[k] * src[f, k]
                qf[s, f, k + 1] = q
                store_edges(rnd, f * levels + k, q)

    def prepare_backward(src, s, rnd):
        run_u = zero_plane
        run_v = zero_plane
        zero_row = jnp.zeros((1, LANES), F32)
        for k in reversed(range(levels)):
            run_u = run_u + wet[k] * src[2, k]
            run_v = run_v + wet[k] * src[3, k]
            store_edges(rnd, planes + k, run_v)
            runs[rnd, k] = lane_diff(run_u) + 0.5 * (
                row_after(run_v, zero_row) - row_before(run_v, zero_row)
            )
        tot_out[rnd] = runs[rnd, 0]
        diag_out[rnd, 0] = run_v[0:1]
        diag_out[rnd, 1] = run_v[rows - 1 : rows]
        for f in range(4):
            for k in range(levels):
                a = wet[k] * src[f, k]
                act[s, f, k] = a
                q = gw[k] * a
                qb[s, f, k + 1] = q
                store_edges(rnd, f * levels + k, q)

    def remote(src, dst, send, recv, to_tile, to_depth):
        return pltpu.make_async_remote_copy(
            src_ref=src,
            dst_ref=dst,
            send_sem=send,
            recv_sem=recv,
            device_id=(to_tile, to_depth),
            device_id_type=MESH,
        )

    def level_up(q, s, rnd):
        return remote(
            q.at[s, :, levels], q.at[s, :, 0], q_send.at[1], q_recv.at[rnd, 0], t, d + 1
        )

    def level_down(q, s, rnd):
        return remote(
            q.at[s, :, 1], q.at[s, :, levels + 1], q_send.at[0], q_recv.at[rnd, 1], t, d - 1
        )

    def edge_copy(rnd, side):
        return remote(
            edge_out.at[rnd, side],
            edge_in.at[rnd, 1 - side],
            e_send.at[side],
            e_recv.at[rnd, 1 - side],
            t - 1 if side == 0 else t + 1,
            d,
        )

    def tot_copy(rnd, peer, slot):
        return remote(
            tot_out.at[rnd], tot_in.at[rnd, slot], t_send.at[0], t_recv.at[rnd, slot], t, peer
        )

    def diag_copy(rnd, side, peer, slot):
        return remote(
            diag_out.at[rnd, side],
            diag_in.at[rnd, 1 - side, slot],
            d_send.at[side],
            d_recv.at[rnd, 1 - side, slot],
            t - 1 if side == 0 else t + 1,
            peer,
        )

    has_side = (t > 0, t < tiles - 1)

    def ahead(forward):
        return (d + 1, depths) if forward else (0, d)

    def behind(forward):
        return (0, d) if forward else (d + 1, depths)

    def send_round(q, s, rnd, forward):
        @pl.when(d < depths - 1)
        def _():
            level_up(q, s, rnd).start()

        @pl.when(d > 0)
        def _():
            level_down(q, s, rnd).start()

        def one(peer, _):
            tot_copy(rnd, peer, d).start()
            for side in range(2):

                @pl.when(has_side[side])
                def _():
                    diag_copy(rnd, side, peer, d).start()

            return 0

        for side in range(2):

            @pl.when(has_side[side])
            def _():
                edge_copy(rnd, side).start()

        lax.fori_loop(*ahead(forward), one, 0)

    def recv_round(q, s, rnd, forward):
        def one(peer, _):
            tot_copy(rnd, peer, peer).wait_recv()
            for side in range(2):

                @pl.when(has_side[1 - side])
                def _():
                    diag_copy(rnd, side, peer, peer).wait_recv()

            return 0

        lax.fori_loop(*behind(forward), one, 0)
        for side in range(2):

            @pl.when(has_side[1 - side])
            def _():
                edge_copy(rnd, side).wait_recv()

        @pl.when(d > 0)
        def _():
            level_up(q, s, rnd).wait_recv()

        @pl.when(d < depths - 1)
        def _():
            level_down(q, s, rnd).wait_recv()

    def drain(part, sem):
        pltpu.make_async_copy(part, part, sem).wait()

    def drain_rounds():
        others = pl.ds(0, depths - 1)
        drain(tot_in.at[pl.ds(0, 2), others], t_send.at[0])
        for side in range(2):

            @pl.when(has_side[side])
            def _():
                drain(edge_in.at[:, side], e_send.at[side])
                drain(diag_in.at[pl.ds(0, 2), side, others], d_send.at[side])

        for way, there in ((0, d > 0), (1, d < depths - 1)):

            @pl.when(there)
            def _():
                drain(qf.at[0, :, pl.ds(1, 4)], q_send.at[way])

    def base_sums(rnd, forward):
        def one(peer, carry):
            base, top, low = carry
            return (
                base + tot_in[rnd, peer],
                top + diag_in[rnd, 0, peer],
                low + diag_in[rnd, 1, peer],
            )

        zero_row = jnp.zeros((1, LANES), F32)
        return lax.fori_loop(*behind(forward), one, (zero_plane, zero_row, zero_row))

    def mixed(q, s, rnd, f, k):
        c = q[s, f, k + 1]
        at = f * levels + k
        north = row_after(c, edge_in[rnd, 1, at : at + 1])
        south = row_before(c, edge_in[rnd, 0, at : at + 1])
        horizontal = (
            north + south + pltpu.roll(c, 1, 1) + pltpu.roll(c, LANES - 1, 1) - 4.0 * c
        )
        vertical = q[s, f, k + 2] + q[s, f, k] - 2.0 * c
        return gw[k] * (nu_horiz * horizontal + nu_vert * vertical)

    row_ids = (t * rows + iota((rows, LANES), 0)).astype(F32)
    coriolis = 0.4 * jnp.sin(math.pi * ((row_ids + 0.5) / (tiles * rows) - 0.5))

    def finish_forward(src, s, rnd, store):
        base, top, low = base_sums(rnd, True)
        for k in range(levels):
            at = planes + k
            p = grav_step * (base + runs[rnd, k])
            p_top = grav_step * (top + edge_in[rnd, 0, at : at + 1])
            p_low = grav_step * (low + edge_in[rnd, 1, at : at + 1])
            gy = 0.5 * (row_after(p, p_low) - row_before(p, p_top))
            w = wet[k]
            for f in range(2):
                store(f, k, w * (src[f, k] + mixed(qf, s, rnd, f, k)))
            u, v = src[2, k], src[3, k]
            store(2, k, w * (u + mixed(qf, s, rnd, 2, k) + coriolis * v - press_coef * lane_diff(p)))
            store(3, k, w * (v + mixed(qf, s, rnd, 3, k) - coriolis * u - press_coef * gy))

    def finish_backward(s, rnd, store):
        base, top, low = base_sums(rnd, False)
        for k in range(levels):
            at = planes + k
            v_top = top + edge_in[rnd, 0, at : at + 1]
            v_low = low + edge_in[rnd, 1, at : at + 1]
            row = iota((rows, LANES), 0)
            rim = jnp.where(row == 0, -0.5 * v_top, 0.0) + jnp.where(row == rows - 1, 0.5 * v_low, 0.0)
            dens = (grav_step * press_coef) * (base + runs[rnd, k] + rim)
            a_t, a_s, a_u, a_v = (act[s, f, k] for f in range(4))
            store(0, k, a_t + mixed(qb, s, rnd, 0, k) - expan[k] * dens)
            store(1, k, a_s + mixed(qb, s, rnd, 1, k) + contr[k] * dens)
            store(2, k, a_u + mixed(qb, s, rnd, 2, k) - coriolis * a_v)
            store(3, k, a_v + mixed(qb, s, rnd, 3, k) + coriolis * a_u)

    prepare_forward(pert, 0, 0)

    sides = has_side[0].astype(I32) + has_side[1].astype(I32)
    pl.semaphore_wait(barrier, (depths - 1) * (1 + sides) + tiles - 1)

    send_round(qf, 0, 0, True)
    loaded(1)
    prepare_backward(cot, 0, 1)
    send_round(qb, 0, 1, False)
    loaded(8, 7, 9, 10)

    own_ids = iota((tiles, LANES), 0)

    def rank_inputs(i, before):
        hot = (owns[pl.ds(i, 1), :] == own_ids).astype(F32)
        at = pl.multiple_of(i * tiles, tiles)
        rank_in[pl.ds(at, tiles), 0:LANES] = hot.astype(BF16)
        rank_in[pl.ds(at, tiles), LANES : 2 * LANES] = before.astype(BF16)
        return before + hot

    lax.fori_loop(0, chunks, rank_inputs, jnp.zeros((tiles, LANES), F32))
    i_row, i_col = iota((2 * LANES, LANES), 0), iota((2 * LANES, LANES), 1)
    earlier = jnp.where((i_row < i_col) | (i_row >= LANES), 1.0, 0.0).astype(BF16)
    ranks[...] = jnp.dot(rank_in[...], earlier, preferred_element_type=F32)
    slot_ids = iota((cap, LANES), 0)

    def slot_inputs(i, _):
        hot = (owns[pl.ds(i, 1), :] == own_ids).astype(F32)
        at = pl.multiple_of(i * tiles, tiles)
        lanes = pl.ds(pl.multiple_of(i * LANES, LANES), LANES)
        rank = jnp.sum(hot * ranks[pl.ds(at, tiles), :], axis=0, keepdims=True).astype(I32)
        hot_rank[:, lanes] = (slot_ids == rank).astype(F32).astype(BF16)
        c = cols[pl.ds(i, 1), :]
        lane = (c & (LANES - 1)).astype(F32)
        row = ((c >> 7) + 32).astype(F32)
        lev = (starts[pl.ds(i, 1), :] * 16 + counts[pl.ds(i, 1), :] - 1).astype(F32)
        hot_own[0:tiles, lanes] = (hot * lane).astype(BF16)
        hot_own[tiles : 2 * tiles, lanes] = (hot * row).astype(BF16)
        hot_own[2 * tiles : 3 * tiles, lanes] = (hot * lev).astype(BF16)
        return 0

    lax.fori_loop(0, chunks, slot_inputs, 0)
    table = lax.dot_general(
        hot_own[...], hot_rank[...], (((1,), (1,)), ((), ())), preferred_element_type=F32
    ).astype(I32)
    for h in range(halves):
        part = table[:, h * LANES : (h + 1) * LANES]
        lane_tab[h * tiles : (h + 1) * tiles] = part[0:tiles]
        row_tab[h * tiles : (h + 1) * tiles] = part[tiles : 2 * tiles] - 32
        lev_tab[h * tiles : (h + 1) * tiles] = part[2 * tiles : 3 * tiles]

    def store_mid(f, k, value):
        mid[f, k] = value

    def store_fin(f, k, value):
        fin_out[f, k] = value
        fin[(f * levels + k) * rows : (f * levels + k + 1) * rows] = value

    def store_amid(f, k, value):
        amid[f, k] = value

    def store_adj(f, k, value):
        adj_out[f, k] = value

    recv_round(qf, 0, 0, True)
    finish_forward(pert, 0, 0, store_mid)
    prepare_forward(mid, 1, 2)
    send_round(qf, 1, 2, True)
    recv_round(qb, 0, 1, False)
    finish_backward(0, 1, store_amid)
    prepare_backward(amid, 1, 3)
    send_round(qb, 1, 3, False)
    recv_round(qf, 1, 2, True)
    finish_forward(mid, 1, 2, store_fin)

    keep_fin = pltpu.make_async_copy(fin_out, fin_hbm, out_sem.at[0])
    keep_fin.start()

    groups = planes // 8
    for g in range(groups):
        for r in range(rows):
            cells[r, g * 8 : g * 8 + 8] = fin[pl.ds(g * 8 * rows + r, 8, stride=rows), :]

    sub = iota((8, LANES), 0)
    level_ids = d * levels + lax.rem(sub, levels)

    def profile_copy(owner):
        return remote(
            send_buf.at[owner],
            prof_out.at[:, pl.ds(pl.multiple_of(t * cap, LANES), cap)],
            p_sem.at[0],
            p_sem.at[1],
            owner,
            d,
        )

    def gather_owner(j, _):
        owner = lax.rem(t + j, tiles)
        for h in range(halves):
            at = pl.ds(h * tiles + owner, 1)
            lane = jnp.broadcast_to(lane_tab[at, :], (8, LANES))
            row = jnp.broadcast_to(row_tab[at, :], (8, LANES))
            lev = jnp.broadcast_to(lev_tab[at, :], (8, LANES))
            first = lev >> 4
            kept = (level_ids >= first) & (level_ids <= first + (lev & 15))
            row = jnp.where(kept, row, -1)
            totals = [jnp.zeros((8, LANES), F32)] * groups
            for r in range(rows):
                here = row == r
                for g in range(groups):
                    got = jnp.take_along_axis(
                        cells[r, g * 8 : g * 8 + 8], lane, axis=1, mode="promise_in_bounds"
                    )
                    totals[g] = jnp.where(here, got, totals[g])
            for g in range(groups):
                send_buf[owner, g * 8 : g * 8 + 8, h * LANES : (h + 1) * LANES] = totals[g]

        @pl.when(j < tiles)
        def _():
            profile_copy(owner).start()

        return 0

    first_part, second_part = 1 + tiles * 16 // 32, 1 + tiles * 31 // 32
    lax.fori_loop(1, first_part, gather_owner, 0)
    recv_round(qb, 1, 3, False)
    finish_backward(1, 3, store_adj)

    keep_adj = pltpu.make_async_copy(adj_out, adj_hbm, out_sem.at[1])
    keep_adj.start()

    for k in range(levels):
        total = zero_plane
        for f in range(4):
            total = total + fin_out[f, k] * adj_out[f, k]
        runs[0, k] = total
    pairs = 8 // levels
    for r in range(rows // pairs):
        for k in range(levels):
            for h in range(pairs):
                at = r + h * (rows // pairs)
                sens_cells[r, k * pairs + h : k * pairs + h + 1] = runs[0, k, at : at + 1]

    sub_level = d * levels + sub // pairs
    sub_row = lax.rem(sub, pairs) * (rows // pairs)

    def gather_sens(owner, _):
        for h in range(halves):
            at = pl.ds(h * tiles + owner, 1)
            lane = jnp.broadcast_to(lane_tab[at, :], (8, LANES))
            row = jnp.broadcast_to(row_tab[at, :], (8, LANES)) - sub_row
            lev = jnp.broadcast_to(lev_tab[at, :], (8, LANES))
            first = lev >> 4
            kept = (sub_level >= first) & (sub_level <= first + (lev & 15))
            row = jnp.where(kept, row, -1)
            total = jnp.zeros((8, LANES), F32)
            for r in range(rows // pairs):
                got = jnp.take_along_axis(sens_cells[r], lane, axis=1, mode="promise_in_bounds")
                total = jnp.where(row == r, got, total)
            sens_part[at, :] = sens_scale * jnp.sum(total, axis=0, keepdims=True)
        return 0

    lax.fori_loop(0, tiles, gather_sens, 0, unroll=4)

    def sens_exchange(peer, slot):
        return remote(sens_part, sens_peer.at[slot], x_send.at[1], x_recv.at[slot], t, peer)

    def start_exchange(j, _):
        sens_exchange(lax.rem(d + j, depths), d).start()
        return 0

    def wait_exchange(j, total):
        peer = lax.rem(d + j, depths)
        sens_exchange(peer, peer).wait_recv()
        return total + sens_peer[peer]

    lax.fori_loop(1, depths, start_exchange, 0)
    lax.fori_loop(first_part, second_part, gather_owner, 0)
    total = lax.fori_loop(1, depths, wait_exchange, sens_part[...])
    for o in range(tiles):
        for h in range(halves):
            sens_send[o, :, h * LANES : (h + 1) * LANES] = total[h * tiles + o : h * tiles + o + 1]

    mine = pl.ds(pl.multiple_of(t * cap, LANES), cap)

    def sens_copy(owner):
        return remote(
            sens_send.at[owner], sens_out.at[:, mine], s_sem.at[0], s_sem.at[1], owner, d
        )

    def start_sens(j, _):
        sens_copy(lax.rem(t + j, tiles)).start()
        return 0

    lax.fori_loop(1, tiles, start_sens, 0)
    own_sens = pltpu.make_async_copy(sens_send.at[t], sens_out.at[:, mine], x_recv.at[d])
    own_sens.start()
    lax.fori_loop(second_part, tiles + 1, gather_owner, 0)
    own_copy = pltpu.make_async_copy(
        send_buf.at[t],
        prof_out.at[:, pl.ds(pl.multiple_of(t * cap, LANES), cap)],
        x_send.at[0],
    )
    own_copy.start()


    drain_rounds()

    drain(sens_peer.at[pl.ds(0, depths - 1)], x_send.at[1])
    keep_fin.wait()
    keep_adj.wait()
    own_copy.wait()
    own_sens.wait()
    for buf, sems in ((send_buf, p_sem), (sens_send, s_sem)):
        all_but_one = buf.at[pl.ds(0, tiles - 1)]
        for way in range(2):
            pltpu.make_async_copy(all_but_one, all_but_one, sems.at[way]).wait()


def place(fin, adj, sens, prof, fin_out, adj_out, sens_out, prof_out, *scratch):
    fin_held, adj_held, sens_held, tiled, lined, sems = scratch
    planes, width = prof.shape
    slots = width // LANES
    groups = planes // 8

    def copy(i, src, dst):
        made = pltpu.make_async_copy(src, dst, sems.at[i])
        made.start()
        return made

    loads = [
        copy(g, prof.at[pl.ds(g * 8, 8)], tiled.at[pl.ds(g * 8, 8)]) for g in range(groups)
    ]
    passed = ((fin, fin_held, fin_out), (adj, adj_held, adj_out), (sens, sens_held, sens_out))
    loads += [copy(groups + i, src, held) for i, (src, held, _) in enumerate(passed)]
    stores = []
    for i, (_, held, out) in enumerate(passed):
        loads[groups + i].wait()
        stores.append(copy(groups + 3 + i, held, out))
    for g in range(groups):
        loads[g].wait()
        for at in range(slots):
            lined[pl.ds(g * 8 * slots + at, 8, stride=slots), :] = tiled[
                g * 8 : g * 8 + 8, at * LANES : (at + 1) * LANES
            ]
        part = pl.ds(g * 8 * slots, 8 * slots)
        stores.append(copy(groups + 6 + g, lined.at[part], prof_out.at[part]))
    for made in stores:
        made.wait()


def shards(
    perturbation,
    cotangent,
    land_mask,
    bottom_level,
    mix_gain,
    expansion,
    contraction,
    columns,
    owners,
    level_start,
    level_count,
):
    tiles, depths = lax.axis_size("tile"), lax.axis_size("depth")
    levels, rows, width = perturbation.shape[1:]
    cand = columns.shape[0]
    chunks = cand // LANES
    cap = 2 * cand // tiles
    planes = 4 * levels
    edge_rows = -(-(planes + levels) // 8) * 8

    def listed(x):
        return x.reshape(chunks, LANES)

    slots = tiles * cap // LANES
    operands = (
        perturbation,
        cotangent,
        land_mask,
        bottom_level,
        mix_gain,
        expansion,
        contraction,
        listed(columns),
        listed(owners),
        listed(level_start),
        listed(level_count),
    )
    hbm = pl.BlockSpec(memory_space=pltpu.HBM)
    state = (4, levels, rows, width)
    dma = pltpu.SemaphoreType.DMA
    final, adjoint, profiles, sensitivity = pl.pallas_call(
        lambda *refs: kernel(
            tiles, depths, refs[:11], *refs[11:15], refs[18:29], *refs[15:18], *refs[29:]
        ),
        out_shape=(
            jax.ShapeDtypeStruct(state, F32),
            jax.ShapeDtypeStruct(state, F32),
            jax.ShapeDtypeStruct((planes, tiles * cap), F32),
            jax.ShapeDtypeStruct((1, tiles * cap), F32),
        ),
        in_specs=[hbm] * 11,
        out_specs=(hbm,) * 4,
        scratch_shapes=[
            pltpu.VMEM(state, F32),
            pltpu.VMEM(state, F32),
            dma((2,)),
            *[pltpu.VMEM(x.shape, x.dtype) for x in operands],
            dma((11,)),
            pltpu.VMEM((levels, rows, width), F32),
            pltpu.VMEM((levels, rows, width), F32),
            pltpu.VMEM((planes * rows, width), F32),
            pltpu.VMEM(state, F32),
            pltpu.VMEM(state, F32),
            pltpu.VMEM((2,) + state, F32),
            pltpu.VMEM((2, 4, levels + 2, rows, width), F32),
            pltpu.VMEM((2, 4, levels + 2, rows, width), F32),
            pltpu.VMEM((4, levels, rows, width), F32),
            pltpu.VMEM((4, 2, edge_rows, width), F32),
            pltpu.VMEM((4, 2, edge_rows, width), F32),
            pltpu.VMEM((4, rows, width), F32),
            pltpu.VMEM((4, depths, rows, width), F32),
            pltpu.VMEM((4, 2, 1, width), F32),
            pltpu.VMEM((4, 2, depths, 1, width), F32),
            pltpu.VMEM((chunks * tiles, 2 * LANES), BF16),
            pltpu.VMEM((chunks * tiles, LANES), F32),
            pltpu.VMEM((3 * tiles, cand), BF16),
            pltpu.VMEM((cap, cand), BF16),
            pltpu.VMEM((cap // LANES * tiles, LANES), I32),
            pltpu.VMEM((cap // LANES * tiles, LANES), I32),
            pltpu.VMEM((cap // LANES * tiles, LANES), I32),
            pltpu.VMEM((rows, planes, width), F32),
            pltpu.VMEM((rows * levels // 8, 8, width), F32),
            pltpu.VMEM((tiles, planes, cap), F32),
            pltpu.VMEM((cap // LANES * tiles, LANES), F32),
            pltpu.VMEM((depths, cap // LANES * tiles, LANES), F32),
            pltpu.VMEM((tiles, 1, cap), F32),
            dma((2,)),
            dma((4, 2)),
            dma((2,)),
            dma((4, 2)),
            dma((1,)),
            dma((4, depths)),
            dma((2,)),
            dma((4, 2, depths)),
            dma((2,)),
            dma((2,)),
            dma((2,)),
            dma((depths,)),
        ],
        compiler_params=pltpu.CompilerParams(
            collective_id=0, has_side_effects=True, vmem_limit_bytes=VMEM_BYTES
        ),
    )(*operands)
    final, adjoint, sensitivity, profiles = pl.pallas_call(
        place,
        out_shape=(
            jax.ShapeDtypeStruct(state, F32),
            jax.ShapeDtypeStruct(state, F32),
            jax.ShapeDtypeStruct((1, tiles * cap), F32),
            jax.ShapeDtypeStruct((planes * slots, LANES), F32),
        ),
        in_specs=[hbm] * 4,
        out_specs=(hbm,) * 4,
        scratch_shapes=[
            pltpu.VMEM(state, F32),
            pltpu.VMEM(state, F32),
            pltpu.VMEM((1, tiles * cap), F32),
            pltpu.VMEM((planes, tiles * cap), F32),
            pltpu.VMEM((planes * slots, LANES), F32),
            dma((6 + planes // 4,)),
        ],
        compiler_params=pltpu.CompilerParams(vmem_limit_bytes=VMEM_BYTES),
    )(final, adjoint, sensitivity, profiles)
    return final, adjoint, profiles.reshape(4, levels, 1, tiles * cap), sensitivity


def solution(mesh):
    placed = (
        P(None, "depth", "tile", None),
        P(None, "depth", "tile", None),
        P("tile", None),
        P("tile", None),
        P("depth", "tile", None),
        P("depth", "tile", None),
        P("depth", "tile", None),
        P("tile"),
        P("tile", None),
        P("tile"),
        P("tile"),
    )
    return jax.shard_map(
        shards,
        mesh=mesh,
        in_specs=placed,
        out_specs=(
            P(None, "depth", "tile", None),
            P(None, "depth", "tile", None),
            P(None, "depth", "tile", None),
            P("tile", None),
        ),
        check_vma=False,
    )
```

```python
import math

import jax
import jax.numpy as jnp
from jax import lax
from jax.experimental import pallas as pl
from jax.experimental.pallas import tpu as pltpu
from jax.sharding import PartitionSpec as P

STEPS = 2
LANES = 128
VMEM_BYTES = 60 * 1024 * 1024

nu_horiz = 0.06
nu_vert = 0.08
press_coef = 0.1
grav_step = 0.2
sens_scale = 0.2

MESH = pl.DeviceIdType.MESH
F32 = jnp.float32
BF16 = jnp.bfloat16
I32 = jnp.int32


def iota(shape, dim):
    return lax.broadcasted_iota(I32, shape, dim)


def lane_diff(p):
    return 0.5 * (pltpu.roll(p, p.shape[1] - 1, 1) - pltpu.roll(p, 1, 1))


def row_after(p, bottom):
    rows = p.shape[0]
    return jnp.where(iota(p.shape, 0) == rows - 1, bottom, pltpu.roll(p, rows - 1, 0))


def row_before(p, top):
    return jnp.where(iota(p.shape, 0) == 0, top, pltpu.roll(p, 1, 0))


def kernel(
    tiles,
    depths,
    inputs,
    fin_hbm,
    adj_hbm,
    prof_out,
    sens_out,
    held,
    fin_out,
    adj_out,
    out_sem,
    load_sem,
    wet,
    gw,
    fin,
    mid,
    amid,
    act,
    qf,
    qb,
    runs,
    edge_out,
    edge_in,
    tot_out,
    tot_in,
    diag_out,
    diag_in,
    rank_in,
    ranks,
    hot_own,
    hot_rank,
    lane_tab,
    row_tab,
    lev_tab,
    cells,
    sens_cells,
    send_buf,
    sens_part,
    sens_peer,
    sens_send,
    q_send,
    q_recv,
    e_send,
    e_recv,
    t_send,
    t_recv,
    d_send,
    d_recv,
    p_sem,
    s_sem,
    x_send,
    x_recv,
    ready,
):
    pert, cot, land, bottom, gain, expan, contr, cols, owns, starts, counts = held
    loads = [pltpu.make_async_copy(a, b, load_sem.at[i]) for i, (a, b) in enumerate(zip(inputs, held))]
    for i in (2, 3, 4, 0, 5, 6, 1, 8, 7, 9, 10):
        loads[i].start()
    levels, rows = wet.shape[0], wet.shape[1]
    cap = hot_rank.shape[0]
    halves = cap // LANES
    chunks = owns.shape[0]
    planes = 4 * levels
    t = lax.axis_index("tile")
    d = lax.axis_index("depth")

    barrier = pltpu.get_barrier_semaphore()

    def greet(to_tile, to_depth):
        pl.semaphore_signal(barrier, inc=1, device_id=(to_tile, to_depth), device_id_type=MESH)

    def greet_depths(j, _):
        peer = lax.rem(d + j, depths)
        greet(t, peer)

        @pl.when(t > 0)
        def _():
            greet(t - 1, peer)

        @pl.when(t < tiles - 1)
        def _():
            greet(t + 1, peer)

        return 0

    lax.fori_loop(1, depths, greet_depths, 0)

    for side, there in ((t - 1, t > 0), (t + 1, t < tiles - 1)):

        @pl.when(there)
        def _():
            greet(side, d)

    across = 8 if tiles % 8 == 0 else 2
    down = tiles // across
    my_row, my_col = t // across, lax.rem(t, across)

    def in_column(j):
        return lax.rem(my_row + j, down) * across + my_col

    def in_row(j):
        return my_row * across + lax.rem(my_col + j, across)

    def greet_column(j, _):
        greet(in_column(j), d)
        return 0

    def greet_row(j, _):
        greet(in_row(j), d)
        return 0

    lax.fori_loop(1, down, greet_column, 0)
    lax.fori_loop(1, across, greet_row, 0)

    zero_plane = jnp.zeros((rows, LANES), F32)

    def loaded(*which):
        for i in which:
            loads[i].wait()

    loaded(2, 3, 4, 0, 5, 6)
    ocean = land[...] == 1
    for k in range(levels):
        w = jnp.where(ocean & (d * levels + k < bottom[...]), 1.0, 0.0).astype(F32)
        wet[k] = w
        gw[k] = w * gain[k]

    @pl.when(d == 0)
    def _():
        for s in range(2):
            for f in range(4):
                qf[s, f, 0] = zero_plane
                qb[s, f, 0] = zero_plane

    @pl.when(d == depths - 1)
    def _():
        for s in range(2):
            for f in range(4):
                qf[s, f, levels + 1] = zero_plane
                qb[s, f, levels + 1] = zero_plane

    def clear_side(side):
        for rnd in range(4):
            edge_in[rnd, side] = jnp.zeros(edge_in.shape[2:], F32)
            diag_in[rnd, side] = jnp.zeros(diag_in.shape[2:], F32)

    @pl.when(t == 0)
    def _():
        clear_side(0)

    @pl.when(t == tiles - 1)
    def _():
        clear_side(1)

    def store_edges(rnd, at, plane):
        edge_out[rnd, 0, at : at + 1] = plane[0:1]
        edge_out[rnd, 1, at : at + 1] = plane[rows - 1 : rows]

    def prepare_forward(src, s, rnd):
        running = zero_plane
        for k in range(levels):
            running = running + (contr[k] * src[1, k] - expan[k] * src[0, k])
            runs[rnd, k] = running
            store_edges(rnd, planes + k, running)
        tot_out[rnd] = running
        diag_out[rnd, 0] = running[0:1]
        diag_out[rnd, 1] = running[rows - 1 : rows]
        for f in range(4):
            for k in range(levels):
                q = gw[k] * src[f, k]
                qf[s, f, k + 1] = q
                store_edges(rnd, f * levels + k, q)

    def prepare_backward(src, s, rnd):
        run_u = zero_plane
        run_v = zero_plane
        zero_row = jnp.zeros((1, LANES), F32)
        for k in reversed(range(levels)):
            run_u = run_u + wet[k] * src[2, k]
            run_v = run_v + wet[k] * src[3, k]
            store_edges(rnd, planes + k, run_v)
            runs[rnd, k] = lane_diff(run_u) + 0.5 * (
                row_after(run_v, zero_row) - row_before(run_v, zero_row)
            )
        tot_out[rnd] = runs[rnd, 0]
        diag_out[rnd, 0] = run_v[0:1]
        diag_out[rnd, 1] = run_v[rows - 1 : rows]
        for f in range(4):
            for k in range(levels):
                a = wet[k] * src[f, k]
                act[s, f, k] = a
                q = gw[k] * a
                qb[s, f, k + 1] = q
                store_edges(rnd, f * levels + k, q)

    def remote(src, dst, send, recv, to_tile, to_depth):
        return pltpu.make_async_remote_copy(
            src_ref=src,
            dst_ref=dst,
            send_sem=send,
            recv_sem=recv,
            device_id=(to_tile, to_depth),
            device_id_type=MESH,
        )

    def level_up(q, s, rnd):
        return remote(
            q.at[s, :, levels], q.at[s, :, 0], q_send.at[1], q_recv.at[rnd, 0], t, d + 1
        )

    def level_down(q, s, rnd):
        return remote(
            q.at[s, :, 1], q.at[s, :, levels + 1], q_send.at[0], q_recv.at[rnd, 1], t, d - 1
        )

    def edge_copy(rnd, side):
        return remote(
            edge_out.at[rnd, side],
            edge_in.at[rnd, 1 - side],
            e_send.at[side],
            e_recv.at[rnd, 1 - side],
            t - 1 if side == 0 else t + 1,
            d,
        )

    def tot_copy(rnd, peer, slot):
        return remote(
            tot_out.at[rnd], tot_in.at[rnd, slot], t_send.at[0], t_recv.at[rnd, slot], t, peer
        )

    def diag_copy(rnd, side, peer, slot):
        return remote(
            diag_out.at[rnd, side],
            diag_in.at[rnd, 1 - side, slot],
            d_send.at[side],
            d_recv.at[rnd, 1 - side, slot],
            t - 1 if side == 0 else t + 1,
            peer,
        )

    has_side = (t > 0, t < tiles - 1)

    def ahead(forward):
        return (d + 1, depths) if forward else (0, d)

    def behind(forward):
        return (0, d) if forward else (d + 1, depths)

    def send_round(q, s, rnd, forward):
        @pl.when(d < depths - 1)
        def _():
            level_up(q, s, rnd).start()

        @pl.when(d > 0)
        def _():
            level_down(q, s, rnd).start()

        def one(peer, _):
            tot_copy(rnd, peer, d).start()
            for side in range(2):

                @pl.when(has_side[side])
                def _():
                    diag_copy(rnd, side, peer, d).start()

            return 0

        for side in range(2):

            @pl.when(has_side[side])
            def _():
                edge_copy(rnd, side).start()

        lax.fori_loop(*ahead(forward), one, 0)

    def recv_round(q, s, rnd, forward):
        def one(peer, _):
            tot_copy(rnd, peer, peer).wait_recv()
            for side in range(2):

                @pl.when(has_side[1 - side])
                def _():
                    diag_copy(rnd, side, peer, peer).wait_recv()

            return 0

        lax.fori_loop(*behind(forward), one, 0)
        for side in range(2):

            @pl.when(has_side[1 - side])
            def _():
                edge_copy(rnd, side).wait_recv()

        @pl.when(d > 0)
        def _():
            level_up(q, s, rnd).wait_recv()

        @pl.when(d < depths - 1)
        def _():
            level_down(q, s, rnd).wait_recv()

    def drain(part, sem):
        pltpu.make_async_copy(part, part, sem).wait()

    def drain_rounds():
        others = pl.ds(0, depths - 1)
        drain(tot_in.at[pl.ds(0, 2), others], t_send.at[0])
        for side in range(2):

            @pl.when(has_side[side])
            def _():
                drain(edge_in.at[:, side], e_send.at[side])
                drain(diag_in.at[pl.ds(0, 2), side, others], d_send.at[side])

        for way, there in ((0, d > 0), (1, d < depths - 1)):

            @pl.when(there)
            def _():
                drain(qf.at[0, :, pl.ds(1, 4)], q_send.at[way])

    def base_sums(rnd, forward):
        def one(peer, carry):
            base, top, low = carry
            return (
                base + tot_in[rnd, peer],
                top + diag_in[rnd, 0, peer],
                low + diag_in[rnd, 1, peer],
            )

        zero_row = jnp.zeros((1, LANES), F32)
        return lax.fori_loop(*behind(forward), one, (zero_plane, zero_row, zero_row))

    def mixed(q, s, rnd, f, k):
        c = q[s, f, k + 1]
        at = f * levels + k
        north = row_after(c, edge_in[rnd, 1, at : at + 1])
        south = row_before(c, edge_in[rnd, 0, at : at + 1])
        horizontal = (
            north + south + pltpu.roll(c, 1, 1) + pltpu.roll(c, LANES - 1, 1) - 4.0 * c
        )
        vertical = q[s, f, k + 2] + q[s, f, k] - 2.0 * c
        return gw[k] * (nu_horiz * horizontal + nu_vert * vertical)

    row_ids = (t * rows + iota((rows, LANES), 0)).astype(F32)
    coriolis = 0.4 * jnp.sin(math.pi * ((row_ids + 0.5) / (tiles * rows) - 0.5))

    def finish_forward(src, s, rnd, store):
        base, top, low = base_sums(rnd, True)
        for k in range(levels):
            at = planes + k
            p = grav_step * (base + runs[rnd, k])
            p_top = grav_step * (top + edge_in[rnd, 0, at : at + 1])
            p_low = grav_step * (low + edge_in[rnd, 1, at : at + 1])
            gy = 0.5 * (row_after(p, p_low) - row_before(p, p_top))
            w = wet[k]
            for f in range(2):
                store(f, k, w * (src[f, k] + mixed(qf, s, rnd, f, k)))
            u, v = src[2, k], src[3, k]
            store(2, k, w * (u + mixed(qf, s, rnd, 2, k) + coriolis * v - press_coef * lane_diff(p)))
            store(3, k, w * (v + mixed(qf, s, rnd, 3, k) - coriolis * u - press_coef * gy))

    def finish_backward(s, rnd, store):
        base, top, low = base_sums(rnd, False)
        for k in range(levels):
            at = planes + k
            v_top = top + edge_in[rnd, 0, at : at + 1]
            v_low = low + edge_in[rnd, 1, at : at + 1]
            row = iota((rows, LANES), 0)
            rim = jnp.where(row == 0, -0.5 * v_top, 0.0) + jnp.where(row == rows - 1, 0.5 * v_low, 0.0)
            dens = (grav_step * press_coef) * (base + runs[rnd, k] + rim)
            a_t, a_s, a_u, a_v = (act[s, f, k] for f in range(4))
            store(0, k, a_t + mixed(qb, s, rnd, 0, k) - expan[k] * dens)
            store(1, k, a_s + mixed(qb, s, rnd, 1, k) + contr[k] * dens)
            store(2, k, a_u + mixed(qb, s, rnd, 2, k) - coriolis * a_v)
            store(3, k, a_v + mixed(qb, s, rnd, 3, k) + coriolis * a_u)

    prepare_forward(pert, 0, 0)

    sides = has_side[0].astype(I32) + has_side[1].astype(I32)
    pl.semaphore_wait(barrier, (depths - 1) * (1 + sides) + sides + down + across - 2)

    send_round(qf, 0, 0, True)
    loaded(1)
    prepare_backward(cot, 0, 1)
    send_round(qb, 0, 1, False)
    loaded(8, 7, 9, 10)

    def vouch(j, _):
        pl.semaphore_signal(ready, inc=1, device_id=(in_row(j), d), device_id_type=MESH)
        return 0

    lax.fori_loop(1, across, vouch, 0)

    own_ids = iota((tiles, LANES), 0)

    def rank_inputs(i, before):
        hot = (owns[pl.ds(i, 1), :] == own_ids).astype(F32)
        at = pl.multiple_of(i * tiles, tiles)
        rank_in[pl.ds(at, tiles), 0:LANES] = hot.astype(BF16)
        rank_in[pl.ds(at, tiles), LANES : 2 * LANES] = before.astype(BF16)
        return before + hot

    lax.fori_loop(0, chunks, rank_inputs, jnp.zeros((tiles, LANES), F32))
    i_row, i_col = iota((2 * LANES, LANES), 0), iota((2 * LANES, LANES), 1)
    earlier = jnp.where((i_row < i_col) | (i_row >= LANES), 1.0, 0.0).astype(BF16)
    ranks[...] = jnp.dot(rank_in[...], earlier, preferred_element_type=F32)
    slot_ids = iota((cap, LANES), 0)

    def slot_inputs(i, _):
        hot = (owns[pl.ds(i, 1), :] == own_ids).astype(F32)
        at = pl.multiple_of(i * tiles, tiles)
        lanes = pl.ds(pl.multiple_of(i * LANES, LANES), LANES)
        rank = jnp.sum(hot * ranks[pl.ds(at, tiles), :], axis=0, keepdims=True).astype(I32)
        hot_rank[:, lanes] = (slot_ids == rank).astype(F32).astype(BF16)
        c = cols[pl.ds(i, 1), :]
        lane = (c & (LANES - 1)).astype(F32)
        row = ((c >> 7) + 32).astype(F32)
        lev = (starts[pl.ds(i, 1), :] * 16 + counts[pl.ds(i, 1), :] - 1).astype(F32)
        hot_own[0:tiles, lanes] = (hot * lane).astype(BF16)
        hot_own[tiles : 2 * tiles, lanes] = (hot * row).astype(BF16)
        hot_own[2 * tiles : 3 * tiles, lanes] = (hot * lev).astype(BF16)
        return 0

    lax.fori_loop(0, chunks, slot_inputs, 0)
    table = lax.dot_general(
        hot_own[...], hot_rank[...], (((1,), (1,)), ((), ())), preferred_element_type=F32
    ).astype(I32)
    for h in range(halves):
        part = table[:, h * LANES : (h + 1) * LANES]
        lane_tab[h * tiles : (h + 1) * tiles] = part[0:tiles]
        row_tab[h * tiles : (h + 1) * tiles] = part[tiles : 2 * tiles] - 32
        lev_tab[h * tiles : (h + 1) * tiles] = part[2 * tiles : 3 * tiles]

    def store_mid(f, k, value):
        mid[f, k] = value

    def store_fin(f, k, value):
        fin_out[f, k] = value
        fin[(f * levels + k) * rows : (f * levels + k + 1) * rows] = value

    def store_amid(f, k, value):
        amid[f, k] = value

    def store_adj(f, k, value):
        adj_out[f, k] = value

    recv_round(qf, 0, 0, True)
    finish_forward(pert, 0, 0, store_mid)
    prepare_forward(mid, 1, 2)
    send_round(qf, 1, 2, True)
    recv_round(qb, 0, 1, False)
    finish_backward(0, 1, store_amid)
    prepare_backward(amid, 1, 3)
    send_round(qb, 1, 3, False)
    recv_round(qf, 1, 2, True)
    finish_forward(mid, 1, 2, store_fin)

    keep_fin = pltpu.make_async_copy(fin_out, fin_hbm, out_sem.at[0])
    keep_fin.start()

    groups = planes // 8
    for g in range(groups):
        for r in range(rows):
            cells[r, g * 8 : g * 8 + 8] = fin[pl.ds(g * 8 * rows + r, 8, stride=rows), :]

    sub = iota((8, LANES), 0)
    level_ids = d * levels + lax.rem(sub, levels)

    def profile_copy(owner):
        return remote(
            send_buf.at[owner],
            prof_out.at[:, pl.ds(pl.multiple_of(t * cap, LANES), cap)],
            p_sem.at[0],
            p_sem.at[1],
            owner,
            d,
        )

    def gather_owner(j, _):
        owner = lax.rem(t + j, tiles)
        for h in range(halves):
            at = pl.ds(h * tiles + owner, 1)
            lane = jnp.broadcast_to(lane_tab[at, :], (8, LANES))
            row = jnp.broadcast_to(row_tab[at, :], (8, LANES))
            lev = jnp.broadcast_to(lev_tab[at, :], (8, LANES))
            first = lev >> 4
            kept = (level_ids >= first) & (level_ids <= first + (lev & 15))
            row = jnp.where(kept, row, -1)
            totals = [jnp.zeros((8, LANES), F32)] * groups
            for r in range(rows):
                here = row == r
                for g in range(groups):
                    got = jnp.take_along_axis(
                        cells[r, g * 8 : g * 8 + 8], lane, axis=1, mode="promise_in_bounds"
                    )
                    totals[g] = jnp.where(here, got, totals[g])
            for g in range(groups):
                send_buf[owner, g * 8 : g * 8 + 8, h * LANES : (h + 1) * LANES] = totals[g]

        @pl.when(j < tiles)
        def _():
            profile_copy(owner).start()

        return 0

    first_part, second_part = 1 + tiles * 16 // 32, 1 + tiles * 31 // 32
    pl.semaphore_wait(ready, across - 1)
    lax.fori_loop(1, first_part, gather_owner, 0)
    recv_round(qb, 1, 3, False)
    finish_backward(1, 3, store_adj)

    keep_adj = pltpu.make_async_copy(adj_out, adj_hbm, out_sem.at[1])
    keep_adj.start()

    for k in range(levels):
        total = zero_plane
        for f in range(4):
            total = total + fin_out[f, k] * adj_out[f, k]
        runs[0, k] = total
    pairs = 8 // levels
    for r in range(rows // pairs):
        for k in range(levels):
            for h in range(pairs):
                at = r + h * (rows // pairs)
                sens_cells[r, k * pairs + h : k * pairs + h + 1] = runs[0, k, at : at + 1]

    sub_level = d * levels + sub // pairs
    sub_row = lax.rem(sub, pairs) * (rows // pairs)

    def gather_sens(owner, _):
        for h in range(halves):
            at = pl.ds(h * tiles + owner, 1)
            lane = jnp.broadcast_to(lane_tab[at, :], (8, LANES))
            row = jnp.broadcast_to(row_tab[at, :], (8, LANES)) - sub_row
            lev = jnp.broadcast_to(lev_tab[at, :], (8, LANES))
            first = lev >> 4
            kept = (sub_level >= first) & (sub_level <= first + (lev & 15))
            row = jnp.where(kept, row, -1)
            total = jnp.zeros((8, LANES), F32)
            for r in range(rows // pairs):
                got = jnp.take_along_axis(sens_cells[r], lane, axis=1, mode="promise_in_bounds")
                total = jnp.where(row == r, got, total)
            sens_part[at, :] = sens_scale * jnp.sum(total, axis=0, keepdims=True)
        return 0

    lax.fori_loop(0, tiles, gather_sens, 0, unroll=4)

    def sens_exchange(peer, slot):
        return remote(sens_part, sens_peer.at[slot], x_send.at[1], x_recv.at[slot], t, peer)

    def start_exchange(j, _):
        sens_exchange(lax.rem(d + j, depths), d).start()
        return 0

    def wait_exchange(j, total):
        peer = lax.rem(d + j, depths)
        sens_exchange(peer, peer).wait_recv()
        return total + sens_peer[peer]

    lax.fori_loop(1, depths, start_exchange, 0)
    lax.fori_loop(first_part, second_part, gather_owner, 0)
    total = lax.fori_loop(1, depths, wait_exchange, sens_part[...])
    for o in range(tiles):
        for h in range(halves):
            sens_send[o, :, h * LANES : (h + 1) * LANES] = total[h * tiles + o : h * tiles + o + 1]

    mine = pl.ds(pl.multiple_of(t * cap, LANES), cap)

    def sens_copy(owner):
        return remote(
            sens_send.at[owner], sens_out.at[:, mine], s_sem.at[0], s_sem.at[1], owner, d
        )

    def start_sens(j, _):
        sens_copy(lax.rem(t + j, tiles)).start()
        return 0

    lax.fori_loop(1, tiles, start_sens, 0)
    own_sens = pltpu.make_async_copy(sens_send.at[t], sens_out.at[:, mine], x_recv.at[d])
    own_sens.start()
    lax.fori_loop(second_part, tiles + 1, gather_owner, 0)
    own_copy = pltpu.make_async_copy(
        send_buf.at[t],
        prof_out.at[:, pl.ds(pl.multiple_of(t * cap, LANES), cap)],
        x_send.at[0],
    )
    own_copy.start()


    drain_rounds()

    drain(sens_peer.at[pl.ds(0, depths - 1)], x_send.at[1])
    keep_fin.wait()
    keep_adj.wait()
    own_copy.wait()
    own_sens.wait()
    for buf, sems in ((send_buf, p_sem), (sens_send, s_sem)):
        all_but_one = buf.at[pl.ds(0, tiles - 1)]
        for way in range(2):
            pltpu.make_async_copy(all_but_one, all_but_one, sems.at[way]).wait()


def place(fin, adj, sens, prof, fin_out, adj_out, sens_out, prof_out, *scratch):
    fin_held, adj_held, sens_held, tiled, lined, sems = scratch
    planes, width = prof.shape
    slots = width // LANES
    groups = planes // 8

    def copy(i, src, dst):
        made = pltpu.make_async_copy(src, dst, sems.at[i])
        made.start()
        return made

    loads = [
        copy(g, prof.at[pl.ds(g * 8, 8)], tiled.at[pl.ds(g * 8, 8)]) for g in range(groups)
    ]
    passed = ((fin, fin_held, fin_out), (adj, adj_held, adj_out), (sens, sens_held, sens_out))
    loads += [copy(groups + i, src, held) for i, (src, held, _) in enumerate(passed)]
    stores = []
    for i, (_, held, out) in enumerate(passed):
        loads[groups + i].wait()
        stores.append(copy(groups + 3 + i, held, out))
    for g in range(groups):
        loads[g].wait()
        for at in range(slots):
            lined[pl.ds(g * 8 * slots + at, 8, stride=slots), :] = tiled[
                g * 8 : g * 8 + 8, at * LANES : (at + 1) * LANES
            ]
        part = pl.ds(g * 8 * slots, 8 * slots)
        stores.append(copy(groups + 6 + g, lined.at[part], prof_out.at[part]))
    for made in stores:
        made.wait()


def shards(
    perturbation,
    cotangent,
    land_mask,
    bottom_level,
    mix_gain,
    expansion,
    contraction,
    columns,
    owners,
    level_start,
    level_count,
):
    tiles, depths = lax.axis_size("tile"), lax.axis_size("depth")
    levels, rows, width = perturbation.shape[1:]
    cand = columns.shape[0]
    chunks = cand // LANES
    cap = 2 * cand // tiles
    planes = 4 * levels
    edge_rows = -(-(planes + levels) // 8) * 8

    def listed(x):
        return x.reshape(chunks, LANES)

    slots = tiles * cap // LANES
    operands = (
        perturbation,
        cotangent,
        land_mask,
        bottom_level,
        mix_gain,
        expansion,
        contraction,
        listed(columns),
        listed(owners),
        listed(level_start),
        listed(level_count),
    )
    hbm = pl.BlockSpec(memory_space=pltpu.HBM)
    state = (4, levels, rows, width)
    dma = pltpu.SemaphoreType.DMA
    final, adjoint, profiles, sensitivity = pl.pallas_call(
        lambda *refs: kernel(
            tiles, depths, refs[:11], *refs[11:15], refs[18:29], *refs[15:18], *refs[29:]
        ),
        out_shape=(
            jax.ShapeDtypeStruct(state, F32),
            jax.ShapeDtypeStruct(state, F32),
            jax.ShapeDtypeStruct((planes, tiles * cap), F32),
            jax.ShapeDtypeStruct((1, tiles * cap), F32),
        ),
        in_specs=[hbm] * 11,
        out_specs=(hbm,) * 4,
        scratch_shapes=[
            pltpu.VMEM(state, F32),
            pltpu.VMEM(state, F32),
            dma((2,)),
            *[pltpu.VMEM(x.shape, x.dtype) for x in operands],
            dma((11,)),
            pltpu.VMEM((levels, rows, width), F32),
            pltpu.VMEM((levels, rows, width), F32),
            pltpu.VMEM((planes * rows, width), F32),
            pltpu.VMEM(state, F32),
            pltpu.VMEM(state, F32),
            pltpu.VMEM((2,) + state, F32),
            pltpu.VMEM((2, 4, levels + 2, rows, width), F32),
            pltpu.VMEM((2, 4, levels + 2, rows, width), F32),
            pltpu.VMEM((4, levels, rows, width), F32),
            pltpu.VMEM((4, 2, edge_rows, width), F32),
            pltpu.VMEM((4, 2, edge_rows, width), F32),
            pltpu.VMEM((4, rows, width), F32),
            pltpu.VMEM((4, depths, rows, width), F32),
            pltpu.VMEM((4, 2, 1, width), F32),
            pltpu.VMEM((4, 2, depths, 1, width), F32),
            pltpu.VMEM((chunks * tiles, 2 * LANES), BF16),
            pltpu.VMEM((chunks * tiles, LANES), F32),
            pltpu.VMEM((3 * tiles, cand), BF16),
            pltpu.VMEM((cap, cand), BF16),
            pltpu.VMEM((cap // LANES * tiles, LANES), I32),
            pltpu.VMEM((cap // LANES * tiles, LANES), I32),
            pltpu.VMEM((cap // LANES * tiles, LANES), I32),
            pltpu.VMEM((rows, planes, width), F32),
            pltpu.VMEM((rows * levels // 8, 8, width), F32),
            pltpu.VMEM((tiles, planes, cap), F32),
            pltpu.VMEM((cap // LANES * tiles, LANES), F32),
            pltpu.VMEM((depths, cap // LANES * tiles, LANES), F32),
            pltpu.VMEM((tiles, 1, cap), F32),
            dma((2,)),
            dma((4, 2)),
            dma((2,)),
            dma((4, 2)),
            dma((1,)),
            dma((4, depths)),
            dma((2,)),
            dma((4, 2, depths)),
            dma((2,)),
            dma((2,)),
            dma((2,)),
            dma((depths,)),
            pltpu.SemaphoreType.REGULAR,
        ],
        compiler_params=pltpu.CompilerParams(
            collective_id=0, has_side_effects=True, vmem_limit_bytes=VMEM_BYTES
        ),
    )(*operands)
    final, adjoint, sensitivity, profiles = pl.pallas_call(
        place,
        out_shape=(
            jax.ShapeDtypeStruct(state, F32),
            jax.ShapeDtypeStruct(state, F32),
            jax.ShapeDtypeStruct((1, tiles * cap), F32),
            jax.ShapeDtypeStruct((planes * slots, LANES), F32),
        ),
        in_specs=[hbm] * 4,
        out_specs=(hbm,) * 4,
        scratch_shapes=[
            pltpu.VMEM(state, F32),
            pltpu.VMEM(state, F32),
            pltpu.VMEM((1, tiles * cap), F32),
            pltpu.VMEM((planes, tiles * cap), F32),
            pltpu.VMEM((planes * slots, LANES), F32),
            dma((6 + planes // 4,)),
        ],
        compiler_params=pltpu.CompilerParams(vmem_limit_bytes=VMEM_BYTES),
    )(final, adjoint, sensitivity, profiles)
    return final, adjoint, profiles.reshape(4, levels, 1, tiles * cap), sensitivity


def solution(mesh):
    placed = (
        P(None, "depth", "tile", None),
        P(None, "depth", "tile", None),
        P("tile", None),
        P("tile", None),
        P("depth", "tile", None),
        P("depth", "tile", None),
        P("depth", "tile", None),
        P("tile"),
        P("tile", None),
        P("tile"),
        P("tile"),
    )
    return jax.shard_map(
        shards,
        mesh=mesh,
        in_specs=placed,
        out_specs=(
            P(None, "depth", "tile", None),
            P(None, "depth", "tile", None),
            P(None, "depth", "tile", None),
            P("tile", None),
        ),
        check_vma=False,
    )
```
